256 devices in a mesh: seq: 16 (over y, x), enc: 16 (over z, core).
Axes of the slice: x: 4, y: 4, z: 8, core: 2. Of those that a mesh axis runs over, the one named last changes fastest.
Arguments:
- decoder_rows: bfloat16 [16, 2048, 4096], P('enc', 'seq'), may hold values from -6 to 6
- query_weight: bfloat16 [4096, 2048], P(None, 'seq'), may hold values from -0.09375 to 0.09375
- neighbour_states: bfloat16 [256, 128, 896], P('enc'), may hold values from -12 to 12
- key_weight: bfloat16 [896, 2048], P(None, 'seq'), may hold values from -0.1875 to 0.1875
- value_weight: bfloat16 [896, 2048], P(None, 'seq'), may hold values from -0.1875 to 0.1875
- block_owner: int32 [16, 32, 2], replicated, may hold values from 0 to 15, all different within a row; in each aligned block of 32 rows (0 to 31, 32 to 63, ..., all dimensions but the last counted through in order) at most 5 rows name the same one
- block_index: int32 [16, 32, 2], replicated, may hold values from 0 to 15
- output_grad: bfloat16 [16, 2048, 2048], P('enc', None, 'seq'), may hold values from -6 to 6
Outputs:
- attended: bfloat16 [16, 2048, 2048], P('enc', None, 'seq')
- states_grad: bfloat16 [256, 128, 896], P('enc', 'seq')
- key_grad: float32 [896, 2048], P(None, 'seq')
- value_grad: float32 [896, 2048], P(None, 'seq')
The draws below stay inside these ranges and needn't reach their ends.
Inputs may be any that keep to these rules, and one draw needn't show every extreme that they name: `block_owner`: within each sequence no owner is named by more than 5 of its neighbour references; a span's 2 neighbours have different owners.
All inputs are finite; a program needn't handle non-finite values.
Results may differ from the reference program's by a relative error of at most 0.023.
Values may be sent and summed in bfloat16 or wider, within the bound.
No kernel may reach another device: no remote copies, remote signals or barrier semaphores. Data moves between devices by JAX's collectives and lax.ppermute only.
A program may use at most 192 MiB of HBM per device.

```python
import math
import jax
import jax.numpy as jnp
import numpy as np
from jax import lax

D = 4096
HEADS = 16
HD = 128
EW = 896
SPAN = 64
NEIGH = 2
RTOK = 128
GROUPS = 16
GTOK = 2048
SPANS_G = 32
HEAD_DEV = 1
CAP = 5
BLK_DEV = 16
BLOCKS = 256
N_SEQ = 16
N_ENC = 16


def set_ends(drawn, own_key, low, largest):
    place = [jax.random.randint(jax.random.fold_in(own_key, axis), (), 0, length) for axis, length in enumerate(drawn.shape)]
    main_axis = drawn.shape.index(max(drawn.shape))
    next_to = place[:main_axis] + [(place[main_axis] + 1) % drawn.shape[main_axis]] + place[main_axis + 1:]
    return drawn.at[tuple(place)].set(low).at[tuple(next_to)].set(largest)


def shard_levels(key, shape, pieces, smallest, top_value):
    def one(dim, blocks):
        draws = jax.random.uniform(jax.random.fold_in(jax.random.fold_in(key, 6), dim), (blocks,), jnp.float32, smallest / len(pieces), top_value / len(pieces))
        return jnp.repeat(jnp.exp(draws), shape[dim] // blocks).reshape((-1,) + (1,) * (len(shape) - dim - 1))

    loudness = one(*pieces[0])
    for cut in pieces[1:]:
        loudness = loudness * one(*cut)
    return loudness


def deal_out(stream_key, own, number, rows, amount, top, most, skew):
    ranking = jax.random.permutation(stream_key, amount)
    heavy_load, usual = load_shares(amount, rows * top, most, skew, True), load_shares(amount, rows * top, most, skew, False)
    places = jnp.arange(amount)

    def named(sizes, rotation):
        used = int((sizes > 0).sum())
        fixed = max(1, used // 4)
        passed = fixed + (places - fixed + rotation * (used - fixed)) % max(1, amount - fixed)
        return jnp.zeros((amount,), jnp.int32).at[ranking[jnp.where(places < fixed, places, passed)]].set(jnp.asarray(sizes, jnp.int32))

    sizes = jnp.where(number % 4 == 0, named(heavy_load, number // 4), named(usual, number - number // 4 - 1))
    mixed = jax.random.permutation(jax.random.fold_in(own, 3), amount)
    source_of, sink = mixed[0:amount // 2 * 2:2], mixed[1:amount // 2 * 2:2]
    slack = jnp.minimum(sizes[source_of] - 1, most - sizes[sink]) // 2
    slack = jnp.where((source_of == ranking[0]) | (sink == ranking[0]) | (sizes[sink] == 0), 0, jnp.maximum(slack, 0))
    passed = jax.random.randint(jax.random.fold_in(own, 4), (amount // 2,), 0, 1 << 20) % (slack + 1)
    sizes = sizes.at[source_of].add(-passed).at[sink].add(passed)
    labels = jnp.searchsorted(jnp.cumsum(sizes), jnp.arange(rows * top), side="right").astype(jnp.int32)
    listing = labels.reshape(top, rows).T
    listing = listing[jax.random.permutation(jax.random.fold_in(own, 1), rows)]
    rotation = jax.random.randint(jax.random.fold_in(own, 2), (rows, 1), 0, top)
    return jnp.take_along_axis(listing, (jnp.arange(top)[None, :] + rotation) % top, axis=1)


def load_shares(number_of, total, limit, skew, full):
    weights = [(1 << 20) // math.isqrt(grade ** skew) + 1 for grade in range(1, number_of + 1)]
    largest = limit if full else min(limit, max(-(-total // number_of), total * weights[0] // sum(weights)))
    least = 1 if total - largest >= number_of - 1 else 0
    counts, spare = [largest] + [least] * (number_of - 1), total - largest - least * (number_of - 1)
    while spare > 0:
        movable = [i for i in range(1, number_of) if counts[i] < largest] or [i for i in range(1, number_of) if counts[i] < limit]
        mass, budget = sum([weights[i] for i in movable]), spare
        for i in movable:
            extra = min(limit - counts[i], max(1, budget * weights[i] // mass), spare)
            counts[i] = counts[i] + extra
            spare = spare - extra
    return np.array(counts)


def centred(key, dims, width, limit, shards=(), held_as=jnp.bfloat16):
    loudness = shard_levels(key, dims, shards, -0.22, 0.18) if shards else 1.0
    result = jax.random.normal(key, dims, jnp.float32) * width * loudness
    return jnp.minimum(jnp.maximum(result, -limit), limit).astype(held_as)


def setup_inputs(seed: int = 0) -> dict:
    arg_keys = jax.random.split(jax.random.key(seed), 9)
    decoder_rows = centred(arg_keys[0], (GROUPS, GTOK, D), 1.0, 6.0, ((0, 16), (1, 16)))
    query_weight = centred(arg_keys[1], (D, HEADS * HD), D ** -0.5, 0.09375, ((1, 16),))
    neighbour_states = centred(arg_keys[2], (BLOCKS, RTOK, EW), 2.0, 12.0, ((0, 16),))
    key_weight = centred(arg_keys[3], (EW, HEADS * HD), EW ** -0.5, 0.1875, ((1, 16),))
    value_weight = centred(arg_keys[4], (EW, HEADS * HD), EW ** -0.5, 0.1875, ((1, 16),))
    block_owner_keys = jax.random.split(jax.random.fold_in(arg_keys[5], 1), GROUPS * SPANS_G // SPANS_G)
    block_owner_turns = jax.random.permutation(jax.random.fold_in(arg_keys[5], 3), GROUPS * SPANS_G // SPANS_G)
    block_owner = jax.vmap(lambda own, number: deal_out(jax.random.fold_in(arg_keys[5], 2), own, number, SPANS_G, N_ENC, NEIGH, CAP, 2))(block_owner_keys, block_owner_turns).reshape((GROUPS, SPANS_G, NEIGH))
    block_index = set_ends(jax.random.randint(arg_keys[6], (GROUPS, SPANS_G, NEIGH), 0, BLK_DEV), jax.random.fold_in(arg_keys[6], 1), 0, BLK_DEV - 1).astype(jnp.int32)
    output_grad = centred(arg_keys[7], (GROUPS, GTOK, HEADS * HD), 1.0, 6.0, ((0, 16), (2, 16)))
    return {"decoder_rows": decoder_rows, "query_weight": query_weight, "neighbour_states": neighbour_states, "key_weight": key_weight, "value_weight": value_weight, "block_owner": block_owner, "block_index": block_index, "output_grad": output_grad}


def shift_rows(rows):
    filler = jnp.zeros((SPAN - 1, rows.shape[1]), rows.dtype)
    joined = jnp.concatenate([rows[SPAN - 1:], filler], axis=0)
    return joined.reshape(SPANS_G, SPAN, rows.shape[1])

def unshift_rows(blocked):
    flat = blocked.reshape(SPANS_G * SPAN, blocked.shape[2])
    filler = jnp.zeros((SPAN - 1, flat.shape[1]), flat.dtype)
    return jnp.concatenate([filler, flat[:GTOK - SPAN + 1]], axis=0)

def attend(q_rows, grad_rows, near_keys, near_vals):
    head_cols = q_rows.shape[1]
    head_count = head_cols // HD
    factor = 1.0 / math.sqrt(HD)
    queries = shift_rows(q_rows).reshape(SPANS_G, SPAN, head_count, HD).astype(jnp.float32)
    grads = shift_rows(grad_rows).reshape(SPANS_G, SPAN, head_count, HD).astype(jnp.float32)
    keys = near_keys.reshape(SPANS_G, NEIGH * RTOK, head_count, HD).astype(jnp.float32)
    vals = near_vals.reshape(SPANS_G, NEIGH * RTOK, head_count, HD).astype(jnp.float32)
    scores = jnp.einsum('cqhd,ckhd->chqk', queries, keys) * factor
    raised = jnp.exp(scores)
    attn_prob = raised / lax.optimization_barrier(jnp.sum(raised, axis=3, keepdims=True))
    prob_bf = attn_prob.astype(jnp.bfloat16)
    attn_out = jnp.einsum('chqk,ckhd->cqhd', prob_bf.astype(jnp.float32), vals).astype(jnp.bfloat16)
    prob_grad = jnp.einsum('cqhd,ckhd->chqk', grads, vals)
    row_inner = lax.optimization_barrier(jnp.sum(attn_prob * prob_grad, axis=3, keepdims=True))
    score_grad = (attn_prob * (prob_grad - row_inner) * factor).astype(jnp.bfloat16)
    near_kgrad = jnp.einsum('chqk,cqhd->ckhd', score_grad.astype(jnp.float32), queries).astype(jnp.bfloat16)
    near_vgrad = jnp.einsum('chqk,cqhd->ckhd', prob_bf.astype(jnp.float32), grads).astype(jnp.bfloat16)
    attended = unshift_rows(attn_out.reshape(SPANS_G, SPAN, head_cols))
    return (attended, near_kgrad.reshape(SPANS_G * NEIGH, RTOK, head_cols), near_vgrad.reshape(SPANS_G * NEIGH, RTOK, head_cols))

def reference(decoder_rows, query_weight, neighbour_states, key_weight, value_weight, block_owner, block_index, output_grad):
    head_cols = HEAD_DEV * HD
    ref_index = (block_owner * BLK_DEV + block_index).reshape(GROUPS, SPANS_G * NEIGH).astype(jnp.int32)
    flat_states = neighbour_states.reshape(BLOCKS * RTOK, EW)

    def head_group(group_idx):
        offset = group_idx * head_cols
        query_cols = lax.dynamic_slice_in_dim(query_weight, offset, head_cols, 1)
        key_cols = lax.dynamic_slice_in_dim(key_weight, offset, head_cols, 1)
        value_cols = lax.dynamic_slice_in_dim(value_weight, offset, head_cols, 1)
        all_keys = jnp.dot(flat_states, key_cols, preferred_element_type=jnp.float32).astype(jnp.bfloat16).reshape(BLOCKS, RTOK, head_cols)
        all_vals = jnp.dot(flat_states, value_cols, preferred_element_type=jnp.float32).astype(jnp.bfloat16).reshape(BLOCKS, RTOK, head_cols)
        grad_cols = lax.dynamic_slice_in_dim(output_grad, offset, head_cols, 2)

        def one_sequence(inputs):
            seq_rows, seq_grads, seq_refs = inputs
            q_rows = jnp.dot(seq_rows, query_cols, preferred_element_type=jnp.float32).astype(jnp.bfloat16)
            near_keys = jnp.take(all_keys, seq_refs, axis=0)
            near_vals = jnp.take(all_vals, seq_refs, axis=0)
            return attend(q_rows, seq_grads, near_keys, near_vals)
        attended, kgrads, vgrads = lax.map(one_sequence, (decoder_rows, grad_cols, ref_index))
        flat_refs = ref_index.reshape(-1)
        block_kgrad = jnp.zeros((BLOCKS, RTOK, head_cols), jnp.float32).at[flat_refs].add(kgrads.reshape(-1, RTOK, head_cols).astype(jnp.float32)).astype(jnp.bfloat16)
        block_vgrad = jnp.zeros((BLOCKS, RTOK, head_cols), jnp.float32).at[flat_refs].add(vgrads.reshape(-1, RTOK, head_cols).astype(jnp.float32)).astype(jnp.bfloat16)
        kflat = block_kgrad.reshape(BLOCKS * RTOK, head_cols)
        vflat = block_vgrad.reshape(BLOCKS * RTOK, head_cols)
        partial_value = (jnp.dot(kflat, key_cols.T, preferred_element_type=jnp.float32) + jnp.dot(vflat, value_cols.T, preferred_element_type=jnp.float32)).astype(jnp.bfloat16)
        key_part = jnp.dot(flat_states.T, kflat, preferred_element_type=jnp.float32)
        value_part = jnp.dot(flat_states.T, vflat, preferred_element_type=jnp.float32)
        return (attended, partial_value, key_part, value_part)
    attended, partial_value, key_part, value_part = lax.map(head_group, jnp.arange(N_SEQ, dtype=jnp.int32))
    attended = jnp.transpose(attended, (1, 2, 0, 3)).reshape(GROUPS, GTOK, HEADS * HD)
    states_grad = lax.optimization_barrier(jnp.sum(partial_value.astype(jnp.float32), axis=0)).astype(jnp.bfloat16).reshape(BLOCKS, RTOK, EW)
    key_grad = jnp.transpose(key_part, (1, 0, 2)).reshape(EW, HEADS * HD)
    value_grad = jnp.transpose(value_part, (1, 0, 2)).reshape(EW, HEADS * HD)
    return (attended, states_grad, key_grad, value_grad)
```

```python
import functools
import math

import jax
import jax.numpy as jnp
from jax import lax
from jax.experimental import pallas as pl
from jax.experimental.pallas import tpu as pltpu
from jax.sharding import PartitionSpec as P

HD = 128
SPAN = 64
NEIGH = 2
CAP = 5
SIDE = 4
BF = jnp.bfloat16
F32 = jnp.float32
NT = (((1,), (1,)), ((), ()))
TN = (((0,), (0,)), ((), ()))
NN = (((1,), (0,)), ((), ()))


def dot(a, b, dims):
    return lax.dot_general(a, b, dims, preferred_element_type=F32)


def x_perm(shift):
    return [(y * SIDE + x, y * SIDE + (x + shift) % SIDE) for y in range(SIDE) for x in range(SIDE)]


def y_perm(shift):
    return [(y * SIDE + x, ((y + shift) % SIDE) * SIDE + x) for y in range(SIDE) for x in range(SIDE)]


def core_perm():
    return [(i, i ^ 1) for i in range(16)]


def kernel_a(core_ref, qo_ref, mine_ref, other_ref, st_ref, pd_ref, part_ref, acc_ref):
    step = pl.program_id(0)
    factor = 1.0 / math.sqrt(HD)
    first = core_ref[0] == 0
    qp, op = [], []
    for j in range(SIDE):
        m = mine_ref[j, 0]
        o = other_ref[j, 0]
        wk = jnp.where(first, m, o)
        wv = jnp.where(first, o, m)
        qp.append(dot(qo_ref[0, 0, j], wk, NT).astype(BF))
        op.append(dot(qo_ref[0, 1, j], wv, NT).astype(BF))

    @pl.when(step == 0)
    def _():
        acc_ref[...] = jnp.zeros_like(acc_ref)

    half = SIDE * SPAN
    for c in range(2):
        rows = slice(c * SPAN, (c + 1) * SPAN)
        qrows = jnp.concatenate([v[rows] for v in qp], axis=0)
        orows = jnp.concatenate([v[rows] for v in op], axis=0)
        keys = st_ref[:, c].reshape(256, st_ref.shape[-1])
        scores = dot(qrows, keys, NT) * factor
        pg = dot(orows, keys, NT)
        raised = jnp.exp(scores)
        prob = raised / jnp.sum(raised, axis=1, keepdims=True)
        inner = jnp.sum(prob * pg, axis=1, keepdims=True)
        pb = prob.astype(BF)
        ds = (prob * (pg - inner) * factor).astype(BF)
        pd_ref[0, c, :half, :] = pb
        pd_ref[0, c, half:, :] = ds
        acc_ref[c] += dot(pb, orows, TN) + dot(ds, qrows, TN)

    @pl.when(step == pl.num_programs(0) - 1)
    def _():
        for c in range(2):
            part_ref[:, c] = acc_ref[c].astype(BF).reshape(16, 16, acc_ref.shape[-1])


def kernel_b(core_ref, pd_ref, qo_ref, mine_ref, other_ref, st_ref, att_ref, gmine_ref, gother_ref):
    first = core_ref[0] == 0
    half = SIDE * SPAN
    ut = []
    for c in range(2):
        keys = st_ref[:, c].reshape(256, st_ref.shape[-1])
        ut.append(dot(pd_ref[0, c], keys, NN).astype(BF))
    for j in range(SIDE):
        rows = slice(j * SPAN, (j + 1) * SPAN)
        trows = slice(half + j * SPAN, half + (j + 1) * SPAN)
        u = jnp.concatenate([ut[0][rows], ut[1][rows]], axis=0)
        t = jnp.concatenate([ut[0][trows], ut[1][trows]], axis=0)
        wv = jnp.where(first, other_ref[j, 0], mine_ref[j, 0])
        att_ref[j, 0] = dot(u, wv, NN).astype(BF)
        vg = dot(u, qo_ref[0, 1, j], TN).astype(BF)
        kg = dot(t, qo_ref[0, 0, j], TN).astype(BF)
        gmine_ref[j, 0] = jnp.where(first, kg, vg)
        gother_ref[j, 0] = jnp.where(first, vg, kg)


def attention(core, qo, mine, other, states):
    width = states.shape[-1]
    qo_spec = pl.BlockSpec((1, 2, SIDE, 128, HD), lambda i, c: (i, 0, 0, 0, 0))
    w_spec = pl.BlockSpec((SIDE, 1, width, HD), lambda i, c: (0, i, 0, 0))
    st_spec = pl.BlockSpec((16, 2, 16, width), lambda i, c: (0, 0, 0, 0))
    pd_spec = pl.BlockSpec((1, 2, 512, 256), lambda i, c: (i, 0, 0, 0))
    params = pltpu.CompilerParams(vmem_limit_bytes=48 * 1024 * 1024)
    pd, part = pl.pallas_call(
        kernel_a,
        grid_spec=pltpu.PrefetchScalarGridSpec(
            num_scalar_prefetch=1,
            grid=(SIDE,),
            in_specs=[qo_spec, w_spec, w_spec, st_spec],
            out_specs=[pd_spec, st_spec],
            scratch_shapes=[pltpu.VMEM((2, 256, width), F32)],
        ),
        out_shape=[
            jax.ShapeDtypeStruct((SIDE, 2, 512, 256), BF),
            jax.ShapeDtypeStruct((16, 2, 16, width), BF),
        ],
        compiler_params=params,
        cost_estimate=pl.CostEstimate(flops=4_700_000_000, bytes_accessed=14 << 20, transcendentals=1 << 19),
        name="attend_a",
    )(core, qo, mine, other, states)
    att, gmine, gother = pl.pallas_call(
        kernel_b,
        grid_spec=pltpu.PrefetchScalarGridSpec(
            num_scalar_prefetch=1,
            grid=(SIDE,),
            in_specs=[pd_spec, qo_spec, w_spec, w_spec, st_spec],
            out_specs=[
                pl.BlockSpec((SIDE, 1, 128, HD), lambda i, c: (0, i, 0, 0)),
                w_spec,
                w_spec,
            ],
        ),
        out_shape=[
            jax.ShapeDtypeStruct((SIDE, SIDE, 128, HD), BF),
            jax.ShapeDtypeStruct((SIDE, SIDE, width, HD), BF),
            jax.ShapeDtypeStruct((SIDE, SIDE, width, HD), BF),
        ],
        compiler_params=params,
        cost_estimate=pl.CostEstimate(flops=3_300_000_000, bytes_accessed=20 << 20, transcendentals=0),
        name="attend_b",
    )(core, pd, qo, mine, other, states)
    return part, att, gmine, gother


def body(rows, wq, states, wk, wv, block_owner, block_index, out_grad):
    s = lax.axis_index("seq")
    e = lax.axis_index("enc")
    y = s // SIDE
    x = s % SIDE
    core = e % 2
    groups = 16
    refs = 64
    width = states.shape[-1]
    four = jnp.arange(SIDE, dtype=jnp.int32)

    owner_all = block_owner.reshape(groups, refs)
    index_all = block_index.reshape(groups, refs)
    owner_hot = (owner_all[:, :, None] == jnp.arange(groups, dtype=jnp.int32)).astype(jnp.int32)
    earlier = jnp.cumsum(owner_hot, axis=1) - owner_hot
    position = jnp.sum(earlier * owner_hot, axis=2)
    slot_ids = jnp.arange(CAP, dtype=jnp.int32)
    matched = (
        (owner_all == e)[:, :, None] & (position[:, :, None] == slot_ids[None, None, :])
    ).astype(jnp.int32)
    send_block = jnp.sum(matched * index_all[:, :, None], axis=1).reshape(-1)
    filled = jnp.sum(matched, axis=1).reshape(-1)
    my_owner = lax.dynamic_index_in_dim(owner_all, e, 0, keepdims=False)
    my_position = lax.dynamic_index_in_dim(position, e, 0, keepdims=False)
    recv_slot = my_owner * CAP + my_position
    slot_hot = (recv_slot[None, :] == jnp.arange(groups * CAP, dtype=jnp.int32)[:, None]).astype(jnp.int32)
    slot_ref = jnp.sum(slot_hot * jnp.arange(refs, dtype=jnp.int32)[None, :], axis=1)

    own_tok = lax.dynamic_slice(states, (0, s * 8, 0), (16, 8, width))
    send = jnp.take(own_tok, send_block, axis=0).reshape(groups, CAP * 8, width)
    got = lax.all_to_all(send, "enc", 0, 0, tiled=True).reshape(groups * CAP, 8, width)
    near = jnp.take(got, recv_slot, axis=0).reshape(groups, 32, width)
    near = lax.all_to_all(near, "seq", 0, 0, tiled=True).reshape(16, 2, 16, width)

    w_mine = lax.all_gather(jnp.where(core == 0, wk, wv), "seq", axis=0, tiled=False)
    w_other = lax.ppermute(w_mine, "enc", core_perm())
    w_mine = w_mine.reshape(SIDE, SIDE, width, HD)
    w_other = w_other.reshape(SIDE, SIDE, width, HD)

    local = rows[0]
    xs = [local] + [lax.ppermute(local, "seq", x_perm(-r)) for r in range(1, SIDE)]
    ws = [wq] + [lax.ppermute(wq, "seq", y_perm(-r)) for r in range(1, SIDE)]
    w_cat = jnp.concatenate(ws, axis=1)
    qrel = jnp.stack([dot(v, w_cat, NN).astype(BF) for v in xs])
    qrel = qrel.reshape(SIDE, 128, SIDE, HD).transpose(2, 0, 1, 3).reshape(16, 128, HD)
    order = (((four - y) % SIDE)[:, None] * SIDE + ((four - x) % SIDE)[None, :]).reshape(-1)
    qabs = jnp.take(qrel, order, axis=0).reshape(SIDE, 512, HD)
    halo = lax.ppermute(qabs[:, :SPAN], "seq", y_perm(-1))
    halo = jnp.where(y == SIDE - 1, jnp.zeros_like(halo), halo)
    qext = jnp.concatenate([qabs, halo], axis=1)
    qwin = jnp.stack([qext[:, 128 * i + SPAN - 1 : 128 * i + SPAN + 127] for i in range(SIDE)])

    og = out_grad[0]
    og = jnp.concatenate([og[SPAN - 1 :], jnp.zeros((SPAN - 1, HD), BF)], axis=0).reshape(SIDE, 512, HD)
    ogr = [lax.dynamic_index_in_dim(og, y, 0, keepdims=False)]
    for r in range(1, SIDE):
        piece = lax.dynamic_index_in_dim(og, (y + r) % SIDE, 0, keepdims=False)
        ogr.append(lax.ppermute(piece, "seq", y_perm(r)))
    oabs = jnp.take(jnp.stack(ogr), (y - four) % SIDE, axis=0)
    owin = oabs.reshape(SIDE, SIDE, 128, HD).transpose(1, 0, 2, 3)
    both = jnp.stack([qwin, owin], axis=1)
    pieces = [lax.dynamic_index_in_dim(both, x, 0, keepdims=False)]
    for r in range(1, SIDE):
        piece = lax.dynamic_index_in_dim(both, (x + r) % SIDE, 0, keepdims=False)
        pieces.append(lax.ppermute(piece, "seq", x_perm(r)))
    qo = jnp.take(jnp.stack(pieces), (x - four) % SIDE, axis=0)

    part, att, gmine, gother = attention(core.reshape(1), qo, w_mine, w_other, near)

    part = lax.all_to_all(part.reshape(16, 32, width), "seq", 0, 0, tiled=True)
    back = jnp.take(part.reshape(refs, 8, width), slot_ref, axis=0).reshape(groups, CAP * 8, width)
    back = lax.all_to_all(back, "enc", 0, 0, tiled=True).reshape(groups * CAP, 8, width)
    block_hot = (
        (send_block[None, :] == jnp.arange(16, dtype=jnp.int32)[:, None]) & (filled[None, :] > 0)
    ).astype(BF)
    states_grad = lax.dot_general(
        block_hot, back, (((1,), (0,)), ((), ())), preferred_element_type=F32
    ).astype(BF)

    att = lax.all_to_all(att.reshape(16, 128, HD), "seq", 0, 0, tiled=True).reshape(2048, HD)
    attended = jnp.concatenate([jnp.zeros((SPAN - 1, HD), BF), att[: 2048 - SPAN + 1]], axis=0)

    gother = lax.ppermute(gother, "enc", core_perm())
    gsum = (gmine.astype(F32) + gother.astype(F32)).astype(BF).reshape(16, width, HD)
    gsum = lax.psum_scatter(gsum, "seq", scatter_dimension=0, tiled=True).reshape(8, width // 8, HD)
    same = [[2 * z for z in range(8)], [2 * z + 1 for z in range(8)]]
    gsum = lax.all_to_all(gsum, "enc", 0, 0, tiled=True, axis_index_groups=same)
    gsum = jnp.sum(gsum.astype(F32), axis=0).astype(BF)
    gall = lax.all_to_all(
        jnp.broadcast_to(gsum[None], (16, width // 8, HD)), "enc", 0, 0, tiled=True
    ).reshape(8, 2, width // 8, HD)
    key_grad = gall[:, 0].reshape(width, HD).astype(F32)
    value_grad = gall[:, 1].reshape(width, HD).astype(F32)
    return attended[None], states_grad, key_grad, value_grad


def solution(mesh):
    placed = (
        P("enc", "seq", None),
        P(None, "seq"),
        P("enc", None, None),
        P(None, "seq"),
        P(None, "seq"),
        P(),
        P(),
        P("enc", None, "seq"),
    )
    return jax.shard_map(
        body,
        mesh=mesh,
        in_specs=placed,
        out_specs=(P("enc", None, "seq"), P("enc", "seq", None), P(None, "seq"), P(None, "seq")),
        check_vma=False,
    )
```

```python
import math

import jax
import jax.numpy as jnp
from jax import lax
from jax.experimental import pallas as pl
from jax.experimental.pallas import tpu as pltpu
from jax.sharding import PartitionSpec as P

HD = 128
SPAN = 64
NEIGH = 2
CAP = 5
SIDE = 4
BF = jnp.bfloat16
F32 = jnp.float32
NT = (((1,), (1,)), ((), ()))
TN = (((0,), (0,)), ((), ()))
NN = (((1,), (0,)), ((), ()))


def dot(a, b, dims):
    return lax.dot_general(a, b, dims, preferred_element_type=F32)


def x_perm(shift):
    return [(y * SIDE + x, y * SIDE + (x + shift) % SIDE) for y in range(SIDE) for x in range(SIDE)]


def y_perm(shift):
    return [(y * SIDE + x, ((y + shift) % SIDE) * SIDE + x) for y in range(SIDE) for x in range(SIDE)]


def pack_kernel(pos_ref, owner_ref, index_ref, tok_ref, out_ref):
    here = pos_ref[1]
    groups, refs = owner_ref.shape
    rows = groups * CAP * 8
    hot = owner_ref[...] == here
    before = lax.broadcasted_iota(jnp.int32, (refs, refs), 0) < lax.broadcasted_iota(jnp.int32, (refs, refs), 1)
    position = dot(hot.astype(BF), before.astype(BF), NN)
    position = jnp.where(hot, position, -1.0).astype(BF)
    row = lax.broadcasted_iota(jnp.int32, (rows, groups), 0)
    group_hot = (row // (CAP * 8) == lax.broadcasted_iota(jnp.int32, (rows, groups), 1)).astype(BF)
    position_row = dot(group_hot, position, NN)
    index_row = dot(group_hot, index_ref[...].astype(BF), NN)
    wide = lax.broadcasted_iota(jnp.int32, (rows, refs), 0)
    slot = ((wide // 8) % CAP).astype(F32)
    block = jnp.sum(jnp.where(position_row == slot, index_row + 1.0, 0.0), axis=1, keepdims=True) - 1.0
    pick_row = lax.broadcasted_iota(jnp.int32, (rows, 128), 0)
    pick_col = lax.broadcasted_iota(jnp.int32, (rows, 128), 1)
    pick = (block == (pick_col // 8).astype(F32)) & (pick_row % 8 == pick_col % 8)
    tok = tok_ref[...].reshape(128, tok_ref.shape[-1])
    out_ref[...] = dot(pick.astype(BF), tok, NN).astype(BF).reshape(out_ref.shape)


def pack(pos, owner, index, states):
    groups, refs = owner.shape
    width = states.shape[-1]
    return pl.pallas_call(
        pack_kernel,
        grid_spec=pltpu.PrefetchScalarGridSpec(
            num_scalar_prefetch=1,
            grid=(1,),
            in_specs=[
                pl.BlockSpec((groups, refs), lambda i, p: (0, 0)),
                pl.BlockSpec((groups, refs), lambda i, p: (0, 0)),
                pl.BlockSpec((16, 8, width), lambda i, p: (0, p[0], 0)),
            ],
            out_specs=pl.BlockSpec((groups, CAP * 8, width), lambda i, p: (0, 0, 0)),
        ),
        out_shape=jax.ShapeDtypeStruct((groups, CAP * 8, width), BF),
        cost_estimate=pl.CostEstimate(flops=150_000_000, bytes_accessed=2 << 20, transcendentals=0),
        name="pack_states",
    )(pos, owner, index, states)


def query_kernel(pos_ref, x0, x1, x2a, x2b, x3, w0, w1, w2a, w2b, w3, out_ref):
    y, x = pos_ref[3], pos_ref[4]
    w2 = jnp.concatenate([w2a[...], w2b[...]], axis=0)
    weights = jnp.concatenate([w0[...], w1[...], w2, w3[...]], axis=1)
    rows = jnp.concatenate([r[...] for r in (x0, x1, x2a, x2b, x3)], axis=0)
    q = dot(rows, weights, NN).astype(BF)
    for k in range(SIDE):
        tok = pl.multiple_of(lax.rem(x + k, SIDE) * 128, 128)
        for n in range(SIDE):
            head = lax.rem(y + n, SIDE)
            out_ref[head, pl.ds(tok, 128), :] = q[128 * k : 128 * (k + 1), HD * n : HD * (n + 1)]


def vmem_call(kernel, outs, name, flops, nbytes, scalars, *arrays, first=()):
    whole = pl.BlockSpec(memory_space=pltpu.VMEM)
    count = 1 + len(arrays)

    def run(*refs):
        kernel(*refs[:count], *refs[count + len(first) :])

    return pl.pallas_call(
        run,
        in_specs=[pl.BlockSpec(memory_space=pltpu.SMEM)]
        + [whole] * len(arrays)
        + [pl.BlockSpec(memory_space=pl.ANY)] * len(first),
        out_specs=[whole] * len(outs),
        out_shape=[jax.ShapeDtypeStruct(shape, dtype) for shape, dtype in outs],
        compiler_params=pltpu.CompilerParams(vmem_limit_bytes=48 * 1024 * 1024),
        cost_estimate=pl.CostEstimate(flops=flops, bytes_accessed=nbytes, transcendentals=0),
        name=name,
    )(scalars, *arrays, *first)


def attend_kernel(pos_ref, qo_ref, *refs):
    mine_ref, other_ref, st_ref, ma_ref, oa_ref, mb_ref, ob_ref, part_ref, acc_ref = refs
    step = pl.program_id(0)
    factor = 1.0 / math.sqrt(HD)
    first = pos_ref[2] == 0
    y = pos_ref[3]
    qs, os, wvs, qp, op = [], [], [], [], []
    for n in range(SIDE):
        j = lax.rem(y + n, SIDE)
        m = mine_ref[j, 0]
        o = other_ref[j, 0]
        wk = jnp.where(first, m, o)
        wvs.append(jnp.where(first, o, m))
        qs.append(qo_ref[0, 0, j])
        os.append(qo_ref[0, 1, j])
        qp.append(dot(qs[n], wk, NT).astype(BF))
        op.append(dot(os[n], wvs[n], NT).astype(BF))

    @pl.when(step == 0)
    def _():
        acc_ref[...] = jnp.zeros_like(acc_ref)

    half = SIDE * SPAN
    ut = []
    for c in range(2):
        rows = slice(c * SPAN, (c + 1) * SPAN)
        lhs = jnp.concatenate([v[rows] for v in qp] + [v[rows] for v in op], axis=0)
        keys = st_ref[:, c].reshape(256, st_ref.shape[-1])
        both = dot(lhs, keys, NT)
        pg = both[half:]
        raised = jnp.exp(both[:half] * factor)
        prob = raised / jnp.sum(raised, axis=1, keepdims=True)
        inner = jnp.sum(prob * pg, axis=1, keepdims=True)
        pb = prob.astype(BF)
        ds = (prob * (pg - inner) * factor).astype(BF)
        ut.append(dot(jnp.concatenate([pb, ds], axis=0), keys, NN).astype(BF))
        acc_ref[c] += dot(jnp.concatenate([ds, pb], axis=0), lhs, TN)

    for n in range(SIDE):
        rows = slice(n * SPAN, (n + 1) * SPAN)
        trows = slice(half + n * SPAN, half + (n + 1) * SPAN)
        u = jnp.concatenate([ut[0][rows], ut[1][rows]], axis=0)
        t = jnp.concatenate([ut[0][trows], ut[1][trows]], axis=0)
        head = lax.rem(y + n, SIDE) * SIDE + lax.rem(pos_ref[4] + step, SIDE)
        part_ref[head, 224:, :] = dot(u, wvs[n], NN).astype(BF)
        vg = dot(os[n], u, TN).astype(BF)
        kg = dot(qs[n], t, TN).astype(BF)
        mine = jnp.where(first, kg, vg)
        other = jnp.where(first, vg, kg)
        ma_ref[0, n] = mine[:SPAN]
        oa_ref[0, n] = other[:SPAN]
        mb_ref[n, 0] = mine[SPAN:]
        ob_ref[n, 0] = other[SPAN:]

    @pl.when(step == pl.num_programs(0) - 1)
    def _():
        for c in range(2):
            for f in range(7):
                rows = slice((c * 7 + f) * 16, (c * 7 + f) * 16 + 16)
                part_ref[:, rows, :] = acc_ref[c, :, f * 128 : (f + 1) * 128].astype(BF).reshape(16, 16, 128)


def attention(pos, qo, mine, other, states):
    width = states.shape[-1]
    w_spec = pl.BlockSpec((SIDE, 1, width, HD), lambda i, c: (0, lax.rem(c[4] + i, SIDE), 0, 0))
    st_spec = pl.BlockSpec((16, 2, 16, width), lambda i, c: (0, 0, 0, 0))
    a_spec = pl.BlockSpec((1, SIDE, SPAN, width), lambda i, c: (i, 0, 0, 0))
    b_spec = pl.BlockSpec((SIDE, 1, SPAN, width), lambda i, c: (0, i, 0, 0))
    grad = jax.ShapeDtypeStruct((SIDE, SIDE, SPAN, width), BF)
    return pl.pallas_call(
        attend_kernel,
        grid_spec=pltpu.PrefetchScalarGridSpec(
            num_scalar_prefetch=1,
            grid=(SIDE,),
            in_specs=[pl.BlockSpec((1, 2, SIDE, 128, HD), lambda i, c: (i, 0, 0, 0, 0))]
            + [w_spec] * 2
            + [st_spec],
            out_specs=[
                a_spec,
                a_spec,
                b_spec,
                b_spec,
                pl.BlockSpec((16, 352, HD), lambda i, c: (0, 0, 0)),
            ],
            scratch_shapes=[pltpu.VMEM((2, 256, width), F32)],
        ),
        out_shape=[
            grad,
            grad,
            grad,
            grad,
            jax.ShapeDtypeStruct((16, 352, HD), BF),
        ],
        compiler_params=pltpu.CompilerParams(vmem_limit_bytes=48 * 1024 * 1024),
        cost_estimate=pl.CostEstimate(flops=8_000_000_000, bytes_accessed=18 << 20, transcendentals=1 << 19),
        name="attend",
    )(pos, qo, *mine, *other, states)


def plane_kernel(pos_ref, *refs):
    outs, tmp = refs[8:12], refs[12]
    tmp[:SPAN] = sum(r[...].astype(F32) for r in refs[:4]).astype(BF)
    tmp[SPAN:] = sum(r[...].astype(F32) for r in refs[4:8]).astype(BF)
    pair = pos_ref[5] // 2
    for k in range(4):
        start = pl.multiple_of(lax.rem(pair + k, 4) * 32, 32)
        outs[k][...] = tmp[pl.ds(start, 32), :]


def plane_sum(pos, parts):
    width = parts[0].shape[-1]
    whole = pl.BlockSpec(memory_space=pltpu.VMEM)
    return pl.pallas_call(
        plane_kernel,
        in_specs=[pl.BlockSpec(memory_space=pltpu.SMEM)] + [whole] * 8,
        out_specs=[whole] * 4,
        out_shape=[jax.ShapeDtypeStruct((32, width), BF)] * 4,
        scratch_shapes=[pltpu.VMEM((128, width), BF)],
        cost_estimate=pl.CostEstimate(flops=20000000000, bytes_accessed=1 << 20, transcendentals=0),
        name="plane_sum",
    )(pos, *parts)


def quarter_kernel(pos_ref, r0, r1, r2, r3, keep_ref, give_ref):
    total = sum(r[...].astype(F32) for r in (r0, r1, r2, r3)).astype(BF)
    even = lax.rem(pos_ref[5], 2) == 0
    keep_ref[...] = jnp.where(even, total[:16], total[16:])
    give_ref[...] = jnp.where(even, total[16:], total[:16])


def eighth_kernel(pos_ref, keep_ref, got_ref, out_ref):
    out_ref[...] = (keep_ref[...].astype(F32) + got_ref[...].astype(F32)).astype(BF)


def pair_kernel(pos_ref, mine_ref, got_ref, out_ref):
    even = lax.rem(pos_ref[5], 2) == 0
    out_ref[:16] = jnp.where(even, mine_ref[...], got_ref[...])
    out_ref[16:] = jnp.where(even, got_ref[...], mine_ref[...])


def join_kernel(pos_ref, r0, r1, r2, r3, out_ref):
    pair = pos_ref[5] // 2
    for k, r in enumerate((r0, r1, r2, r3)):
        start = pl.multiple_of(lax.rem(pair + k, 4) * 32, 32)
        out_ref[pl.ds(start, 32), :] = r[...]


def final_kernel(pos_ref, mine_ref, other_ref, key_ref, value_ref):
    first = pos_ref[2] == 0
    m = mine_ref[...]
    o = other_ref[...]
    key_ref[...] = jnp.where(first, m, o).astype(F32).T
    value_ref[...] = jnp.where(first, o, m).astype(F32).T


def seq_permute(v, perm):
    return lax.ppermute(v, "seq", perm)


def swap(v):
    return lax.ppermute(v, "enc", [(i, i ^ 1) for i in range(16)])


def z_permute(v, shift):
    pairs = [(2 * z + c, 2 * ((z + shift) % 8) + c) for z in range(8) for c in range(2)]
    return lax.ppermute(v, "enc", pairs)


def z_partner(v):
    return lax.ppermute(v, "enc", [(2 * z + c, 2 * (z ^ 1) + c) for z in range(8) for c in range(2)])


def after_kernel(*refs):
    pass


def after(v, *others, flops=0):
    anywhere = pl.BlockSpec(memory_space=pl.ANY)
    return pl.pallas_call(
        after_kernel,
        in_specs=[anywhere] * (1 + len(others)),
        out_specs=anywhere,
        out_shape=jax.ShapeDtypeStruct(v.shape, v.dtype),
        input_output_aliases={0: 0},
        cost_estimate=pl.CostEstimate(flops=flops, bytes_accessed=0, transcendentals=0),
        name="after",
    )(v, *others)


def body(rows, wq, states, wk, wv, block_owner, block_index, out_grad):
    s = lax.axis_index("seq")
    e = lax.axis_index("enc")
    y = s // SIDE
    x = s % SIDE
    core = e % 2
    pos = jnp.stack([s, e, core, y, x, e // 2]).astype(jnp.int32)
    groups = 16
    refs = 64
    width = states.shape[-1]
    four = jnp.arange(SIDE, dtype=jnp.int32)
    owner_all = block_owner.reshape(groups, refs)
    index_all = block_index.reshape(groups, refs)

    x1 = seq_permute(rows[0], x_perm(-1))
    x3 = seq_permute(rows[0], x_perm(1))
    xs = [rows[0], x1, seq_permute(x3[:64], x_perm(1)), seq_permute(x1[64:], x_perm(-1)), x3]
    w1 = seq_permute(wq, y_perm(-1))
    w3 = seq_permute(wq, y_perm(1))
    half = wq.shape[0] // 2
    ws = [wq, w1, seq_permute(w3[:half], y_perm(1)), seq_permute(w1[half:], y_perm(-1)), w3]
    send = pack(pos, owner_all, index_all, states)
    got = lax.all_to_all(send, "enc", 0, 0, tiled=True).reshape(groups * CAP, 8, width)
    og = out_grad[0]
    og = jnp.concatenate([og[SPAN - 1 :], jnp.zeros((SPAN - 1, HD), BF)], axis=0).reshape(SIDE, 512, HD)
    og = after(og, xs[2], xs[3])
    ogr = [lax.dynamic_index_in_dim(og, y, 0, keepdims=False)]
    for r in range(1, SIDE):
        piece = lax.dynamic_index_in_dim(og, (y + r) % SIDE, 0, keepdims=False)
        ogr.append(seq_permute(piece, y_perm(r)))
    oabs = jnp.take(jnp.stack(ogr), (y - four) % SIDE, axis=0)
    owin = oabs.reshape(SIDE, SIDE, 128, HD).transpose(1, 0, 2, 3)

    qabs = vmem_call(
        query_kernel, [((SIDE, 512, HD), BF)], "queries", 13000000000, 9 << 20, pos, *xs, *ws
    )[0]

    w_kind = jnp.where(core == 0, wk, wv)
    w_all = lax.all_gather(w_kind, "seq", axis=0, tiled=False)

    owner_hot = (owner_all[:, :, None] == jnp.arange(groups, dtype=jnp.int32)).astype(jnp.int32)
    earlier = jnp.cumsum(owner_hot, axis=1) - owner_hot
    position = jnp.sum(earlier * owner_hot, axis=2)
    slot_ids = jnp.arange(CAP, dtype=jnp.int32)
    matched = (
        (owner_all == e)[:, :, None] & (position[:, :, None] == slot_ids[None, None, :])
    ).astype(jnp.int32)
    send_block = jnp.sum(matched * index_all[:, :, None], axis=1).reshape(-1)
    filled = jnp.sum(matched, axis=1).reshape(-1)
    my_owner = lax.dynamic_index_in_dim(owner_all, e, 0, keepdims=False)
    my_position = lax.dynamic_index_in_dim(position, e, 0, keepdims=False)
    recv_slot = my_owner * CAP + my_position
    slot_hot = (recv_slot[None, :] == jnp.arange(groups * CAP, dtype=jnp.int32)[:, None]).astype(jnp.int32)
    slot_ref = jnp.sum(slot_hot * jnp.arange(refs, dtype=jnp.int32)[None, :], axis=1)

    near = jnp.take(got, recv_slot, axis=0).reshape(groups, 32, width)
    near_all = lax.all_to_all(near, "seq", 0, 0, tiled=True).reshape(16, 2, 16, width)

    halo = seq_permute(after(qabs[:, :SPAN], near), y_perm(-1))
    halo = jnp.where(y == SIDE - 1, jnp.zeros_like(halo), halo)
    qext = jnp.concatenate([qabs, halo], axis=1)
    qwin = jnp.stack([qext[:, 128 * i + SPAN - 1 : 128 * i + SPAN + 127] for i in range(SIDE)])
    both = jnp.stack([qwin, owin], axis=1)
    pieces = [lax.dynamic_index_in_dim(both, x, 0, keepdims=False)]
    for k in range(1, SIDE):
        piece = lax.dynamic_index_in_dim(both, (x - k) % SIDE, 0, keepdims=False)
        pieces.append(seq_permute(piece, x_perm(-k)))
    w_all = after(w_all, near_all, *pieces[1:])
    w_swap = swap(w_all)
    w_mine = [w_all.reshape(SIDE, SIDE, width, HD)]
    w_other = [w_swap.reshape(SIDE, SIDE, width, HD)]
    qo = jnp.stack(pieces)

    mine_a, other_a, mine_b, other_b, part = attention(pos, qo, w_mine, w_other, near_all)

    part = lax.all_to_all(part, "seq", 0, 0, tiled=True)

    def total(parts):
        return sum(p.astype(F32) for p in parts).astype(BF)

    other_a = swap(other_a)
    other_b = swap(other_b)
    ca = [total([mine_a[k], other_a[k]]) for k in range(SIDE)]
    cb = [total([mine_b[k], other_b[k]]) for k in range(SIDE)]
    ra = [ca[0]] + [seq_permute(ca[k], x_perm(k)) for k in (1, 3, 2)]
    rb = [cb[0]] + [seq_permute(cb[k], y_perm(k)) for k in (1, 3, 2)]

    part = after(part, ca[1], cb[1])
    att = part[:, 224:].reshape(2048, HD)
    attended = jnp.concatenate([jnp.zeros((SPAN - 1, HD), BF), att[: 2048 - SPAN + 1]], axis=0)
    part = part[:, :224].reshape(16, 2, 7, 2, 8, HD).transpose(0, 1, 3, 2, 4, 5).reshape(refs, 56, HD)
    back = jnp.take(part, slot_ref, axis=0).reshape(groups, CAP * 56, HD)
    back = lax.all_to_all(back, "enc", 0, 0, tiled=True).reshape(groups * CAP, 56, HD)
    block_hot = (
        (send_block[None, :] == jnp.arange(16, dtype=jnp.int32)[:, None]) & (filled[None, :] > 0)
    ).astype(BF)
    states_grad = lax.dot_general(block_hot, back, NN, preferred_element_type=F32).astype(BF)
    states_grad = states_grad.reshape(16, 7, 8, HD).transpose(0, 2, 1, 3).reshape(16, 8, width)

    ra, rb = total(ra), total(rb)
    parts = [ra[0]] + [seq_permute(ra[k], y_perm(k)) for k in range(1, SIDE)]
    parts += [rb[0]] + [seq_permute(rb[k], x_perm(k)) for k in range(1, SIDE)]
    slices = plane_sum(pos, parts)
    slices = [slices[0]] + [z_permute(slices[k], 2 * k) for k in range(1, 4)]
    keep, give = vmem_call(quarter_kernel, [((16, width), BF)] * 2, "quarter", 1 << 17, 1 << 18, pos, *slices, first=(back,))
    mine = vmem_call(eighth_kernel, [((16, width), BF)], "eighth", 1 << 17, 1 << 17, pos, keep, z_partner(give))[0]
    mine = vmem_call(pair_kernel, [((32, width), BF)], "pair", 1, 1 << 17, pos, mine, z_partner(mine))[0]
    spread = [mine] + [z_permute(mine, -2 * k) for k in range(1, 4)]
    mine = vmem_call(join_kernel, [((128, width), BF)], "join", 1, 1 << 19, pos, *spread)[0]
    key_grad, value_grad = vmem_call(
        final_kernel, [((width, HD), F32)] * 2, "final", 1, 3 << 19, pos, mine, swap(mine)
    )
    return attended[None], states_grad, key_grad, value_grad


def solution(mesh):
    placed = (
        P("enc", "seq", None),
        P(None, "seq"),
        P("enc", None, None),
        P(None, "seq"),
        P(None, "seq"),
        P(),
        P(),
        P("enc", None, "seq"),
    )
    return jax.shard_map(
        body,
        mesh=mesh,
        in_specs=placed,
        out_specs=(P("enc", None, "seq"), P("enc", "seq", None), P(None, "seq"), P(None, "seq")),
        check_vma=False,
    )
```

```python
import math

import jax
import jax.numpy as jnp
from jax import lax
from jax.experimental import pallas as pl
from jax.experimental.pallas import tpu as pltpu
from jax.sharding import PartitionSpec as P

HD = 128
SPAN = 64
NEIGH = 2
CAP = 5
SIDE = 4
BF = jnp.bfloat16
F32 = jnp.float32
NT = (((1,), (1,)), ((), ()))
TN = (((0,), (0,)), ((), ()))
NN = (((1,), (0,)), ((), ()))


def dot(a, b, dims):
    return lax.dot_general(a, b, dims, preferred_element_type=F32)


def x_perm(shift):
    return [(y * SIDE + x, y * SIDE + (x + shift) % SIDE) for y in range(SIDE) for x in range(SIDE)]


def y_perm(shift):
    return [(y * SIDE + x, ((y + shift) % SIDE) * SIDE + x) for y in range(SIDE) for x in range(SIDE)]


def pack_kernel(pos_ref, owner_ref, index_ref, tok_ref, out_ref):
    here = pos_ref[1]
    groups, refs = owner_ref.shape
    rows = groups * CAP * 8
    hot = owner_ref[...] == here
    before = lax.broadcasted_iota(jnp.int32, (refs, refs), 0) < lax.broadcasted_iota(jnp.int32, (refs, refs), 1)
    position = dot(hot.astype(BF), before.astype(BF), NN)
    position = jnp.where(hot, position, -1.0).astype(BF)
    row = lax.broadcasted_iota(jnp.int32, (rows, groups), 0)
    group_hot = (row // (CAP * 8) == lax.broadcasted_iota(jnp.int32, (rows, groups), 1)).astype(BF)
    position_row = dot(group_hot, position, NN)
    index_row = dot(group_hot, index_ref[...].astype(BF), NN)
    wide = lax.broadcasted_iota(jnp.int32, (rows, refs), 0)
    slot = ((wide // 8) % CAP).astype(F32)
    block = jnp.sum(jnp.where(position_row == slot, index_row + 1.0, 0.0), axis=1, keepdims=True) - 1.0
    pick_row = lax.broadcasted_iota(jnp.int32, (rows, 128), 0)
    pick_col = lax.broadcasted_iota(jnp.int32, (rows, 128), 1)
    pick = (block == (pick_col // 8).astype(F32)) & (pick_row % 8 == pick_col % 8)
    tok = tok_ref[...].reshape(128, tok_ref.shape[-1])
    out_ref[...] = dot(pick.astype(BF), tok, NN).astype(BF).reshape(out_ref.shape)


def pack(pos, owner, index, states):
    groups, refs = owner.shape
    width = states.shape[-1]
    return pl.pallas_call(
        pack_kernel,
        grid_spec=pltpu.PrefetchScalarGridSpec(
            num_scalar_prefetch=1,
            grid=(1,),
            in_specs=[
                pl.BlockSpec((groups, refs), lambda i, p: (0, 0)),
                pl.BlockSpec((groups, refs), lambda i, p: (0, 0)),
                pl.BlockSpec((16, 8, width), lambda i, p: (0, p[0], 0)),
            ],
            out_specs=pl.BlockSpec((groups, CAP * 8, width), lambda i, p: (0, 0, 0)),
        ),
        out_shape=jax.ShapeDtypeStruct((groups, CAP * 8, width), BF),
        cost_estimate=pl.CostEstimate(flops=150_000_000, bytes_accessed=2 << 20, transcendentals=0),
        name="pack_states",
    )(pos, owner, index, states)


def query_kernel(pos_ref, x0, x1, x2a, x2b, x3, own, near, near_other, far, far_other, out_ref, head_ref):
    core, y, x = pos_ref[2], pos_ref[3], pos_ref[4]
    first = core == 0
    low = jnp.where(first, far[...], far_other[...])
    high = jnp.where(first, far_other[...], far[...])
    across = jnp.concatenate([low, high], axis=0)
    weights = jnp.concatenate([own[...], near[...], across, near_other[...]], axis=1)
    rows = jnp.concatenate([r[...] for r in (x0, x1, x2a, x2b, x3)], axis=0)
    q = dot(rows, weights, NN).astype(BF)
    steps = (0, 1 + 2 * core, 2, 3 - 2 * core)
    for k in range(SIDE):
        tok = pl.multiple_of(lax.rem(x + k, SIDE) * 128, 128)
        for n in range(SIDE):
            head = lax.rem(y + steps[n], SIDE)
            out_ref[head, pl.ds(tok, 128), :] = q[128 * k : 128 * (k + 1), HD * n : HD * (n + 1)]
    head_ref[...] = out_ref[:, :SPAN, :]


def window_kernel(pos_ref, q_ref, halo_ref, o0, o1, o2, o3, p0, p1, p2, p3):
    y, x = pos_ref[3], pos_ref[4]
    halo = jnp.where(y == SIDE - 1, 0.0, halo_ref[...].astype(F32))
    for k, out_ref in enumerate((p0, p1, p2, p3)):
        to = lax.rem(x + SIDE - k, SIDE)
        start = pl.multiple_of(to * 128, 128)
        after_start = pl.multiple_of(lax.rem(to + 1, SIDE) * 128, 128)
        for j in range(SIDE):
            block = q_ref[j, pl.ds(start, 128), :].astype(F32)
            following = q_ref[j, pl.ds(after_start, SPAN), :].astype(F32)
            following = jnp.where(to == SIDE - 1, halo[j], following)
            rows = jnp.concatenate([block, following], axis=0)
            out_ref[0, j] = rows[SPAN - 1 : SPAN + 127].astype(BF)
        for r, o_ref in enumerate((o0, o1, o2, o3)):
            out_ref[1, lax.rem(y + SIDE - r, SIDE)] = o_ref[pl.ds(start, 128), :]


def vmem_call(kernel, outs, name, flops, nbytes, scalars, *arrays, first=()):
    whole = pl.BlockSpec(memory_space=pltpu.VMEM)
    count = 1 + len(arrays)

    def run(*refs):
        kernel(*refs[:count], *refs[count + len(first) :])

    return pl.pallas_call(
        run,
        in_specs=[pl.BlockSpec(memory_space=pltpu.SMEM)]
        + [whole] * len(arrays)
        + [pl.BlockSpec(memory_space=pl.ANY)] * len(first),
        out_specs=[whole] * len(outs),
        out_shape=[jax.ShapeDtypeStruct(shape, dtype) for shape, dtype in outs],
        compiler_params=pltpu.CompilerParams(vmem_limit_bytes=48 * 1024 * 1024),
        cost_estimate=pl.CostEstimate(flops=flops, bytes_accessed=nbytes, transcendentals=0),
        name=name,
    )(scalars, *arrays, *first)


def attend_kernel(pos_ref, qo_ref, *refs):
    mine_ref, other_ref, st_ref, ma_ref, oa_ref, mb_ref, ob_ref, part_ref, acc_ref = refs
    step = pl.program_id(0)
    factor = 1.0 / math.sqrt(HD)
    first = pos_ref[2] == 0
    y = pos_ref[3]
    qs, os, wvs, qp, op = [], [], [], [], []
    for n in range(SIDE):
        j = lax.rem(y + n, SIDE)
        m = mine_ref[j, 0]
        o = other_ref[j, 0]
        wk = jnp.where(first, m, o)
        wvs.append(jnp.where(first, o, m))
        qs.append(qo_ref[0, 0, j])
        os.append(qo_ref[0, 1, j])
        qp.append(dot(qs[n], wk, NT).astype(BF))
        op.append(dot(os[n], wvs[n], NT).astype(BF))

    @pl.when(step == 0)
    def _():
        acc_ref[...] = jnp.zeros_like(acc_ref)

    half = SIDE * SPAN
    ut = []
    for c in range(2):
        rows = slice(c * SPAN, (c + 1) * SPAN)
        lhs = jnp.concatenate([v[rows] for v in qp] + [v[rows] for v in op], axis=0)
        keys = st_ref[:, c].reshape(256, st_ref.shape[-1])
        both = dot(lhs, keys, NT)
        pg = both[half:]
        raised = jnp.exp(both[:half] * factor)
        prob = raised / jnp.sum(raised, axis=1, keepdims=True)
        inner = jnp.sum(prob * pg, axis=1, keepdims=True)
        pb = prob.astype(BF)
        ds = (prob * (pg - inner) * factor).astype(BF)
        ut.append(dot(jnp.concatenate([pb, ds], axis=0), keys, NN).astype(BF))
        acc_ref[c] += dot(jnp.concatenate([ds, pb], axis=0), lhs, TN)

    for n in range(SIDE):
        rows = slice(n * SPAN, (n + 1) * SPAN)
        trows = slice(half + n * SPAN, half + (n + 1) * SPAN)
        u = jnp.concatenate([ut[0][rows], ut[1][rows]], axis=0)
        t = jnp.concatenate([ut[0][trows], ut[1][trows]], axis=0)
        head = lax.rem(y + n, SIDE) * SIDE + lax.rem(pos_ref[4] + step, SIDE)
        part_ref[head, 224:, :] = dot(u, wvs[n], NN).astype(BF)
        vg = dot(os[n], u, TN).astype(BF)
        kg = dot(qs[n], t, TN).astype(BF)
        mine = jnp.where(first, kg, vg)
        other = jnp.where(first, vg, kg)
        ma_ref[0, n] = mine[:SPAN]
        oa_ref[0, n] = other[:SPAN]
        mb_ref[n, 0] = mine[SPAN:]
        ob_ref[n, 0] = other[SPAN:]

    @pl.when(step == pl.num_programs(0) - 1)
    def _():
        for c in range(2):
            for f in range(7):
                rows = slice((c * 7 + f) * 16, (c * 7 + f) * 16 + 16)
                part_ref[:, rows, :] = acc_ref[c, :, f * 128 : (f + 1) * 128].astype(BF).reshape(16, 16, 128)


def attention(pos, qo, mine, other, states):
    width = states.shape[-1]
    w_spec = pl.BlockSpec((SIDE, 1, width, HD), lambda i, c: (0, lax.rem(c[4] + i, SIDE), 0, 0))
    st_spec = pl.BlockSpec((16, 2, 16, width), lambda i, c: (0, 0, 0, 0))
    a_spec = pl.BlockSpec((1, SIDE, SPAN, width), lambda i, c: (i, 0, 0, 0))
    b_spec = pl.BlockSpec((SIDE, 1, SPAN, width), lambda i, c: (0, i, 0, 0))
    grad = jax.ShapeDtypeStruct((SIDE, SIDE, SPAN, width), BF)
    return pl.pallas_call(
        attend_kernel,
        grid_spec=pltpu.PrefetchScalarGridSpec(
            num_scalar_prefetch=1,
            grid=(SIDE,),
            in_specs=[pl.BlockSpec((1, 2, SIDE, 128, HD), lambda i, c: (i, 0, 0, 0, 0))]
            + [w_spec] * 2
            + [st_spec],
            out_specs=[
                a_spec,
                a_spec,
                b_spec,
                b_spec,
                pl.BlockSpec((16, 352, HD), lambda i, c: (0, 0, 0)),
            ],
            scratch_shapes=[pltpu.VMEM((2, 256, width), F32)],
        ),
        out_shape=[
            grad,
            grad,
            grad,
            grad,
            jax.ShapeDtypeStruct((16, 352, HD), BF),
        ],
        compiler_params=pltpu.CompilerParams(vmem_limit_bytes=48 * 1024 * 1024),
        cost_estimate=pl.CostEstimate(flops=8_000_000_000, bytes_accessed=18 << 20, transcendentals=1 << 19),
        name="attend",
    )(pos, qo, *mine, *other, states)


def plane_kernel(pos_ref, *refs):
    outs, tmp = refs[8:12], refs[12]
    tmp[:SPAN] = sum(r[...].astype(F32) for r in refs[:4]).astype(BF)
    tmp[SPAN:] = sum(r[...].astype(F32) for r in refs[4:8]).astype(BF)
    pair = pos_ref[5] // 2
    for k in range(4):
        start = pl.multiple_of(lax.rem(pair + k, 4) * 32, 32)
        outs[k][...] = tmp[pl.ds(start, 32), :]


def plane_sum(pos, parts):
    width = parts[0].shape[-1]
    whole = pl.BlockSpec(memory_space=pltpu.VMEM)
    return pl.pallas_call(
        plane_kernel,
        in_specs=[pl.BlockSpec(memory_space=pltpu.SMEM)] + [whole] * 8,
        out_specs=[whole] * 4,
        out_shape=[jax.ShapeDtypeStruct((32, width), BF)] * 4,
        scratch_shapes=[pltpu.VMEM((128, width), BF)],
        cost_estimate=pl.CostEstimate(flops=10000000000, bytes_accessed=1 << 20, transcendentals=0),
        name="plane_sum",
    )(pos, *parts)


def quarter_kernel(pos_ref, r0, r1, r2, r3, keep_ref, give_ref):
    total = sum(r[...].astype(F32) for r in (r0, r1, r2, r3)).astype(BF)
    even = lax.rem(pos_ref[5], 2) == 0
    keep_ref[...] = jnp.where(even, total[:16], total[16:])
    give_ref[...] = jnp.where(even, total[16:], total[:16])


def eighth_kernel(pos_ref, keep_ref, got_ref, out_ref):
    out_ref[...] = (keep_ref[...].astype(F32) + got_ref[...].astype(F32)).astype(BF)


def pair_kernel(pos_ref, mine_ref, got_ref, out_ref):
    even = lax.rem(pos_ref[5], 2) == 0
    out_ref[:16] = jnp.where(even, mine_ref[...], got_ref[...])
    out_ref[16:] = jnp.where(even, got_ref[...], mine_ref[...])


def join_kernel(pos_ref, r0, r1, r2, r3, out_ref):
    pair = pos_ref[5] // 2
    for k, r in enumerate((r0, r1, r2, r3)):
        start = pl.multiple_of(lax.rem(pair + k, 4) * 32, 32)
        out_ref[pl.ds(start, 32), :] = r[...]


def final_kernel(pos_ref, mine_ref, other_ref, key_ref, value_ref):
    first = pos_ref[2] == 0
    m = mine_ref[...]
    o = other_ref[...]
    key_ref[...] = jnp.where(first, m, o).astype(F32).T
    value_ref[...] = jnp.where(first, o, m).astype(F32).T


def seq_permute(v, perm):
    return lax.ppermute(v, "seq", perm)


def swap(v):
    return lax.ppermute(v, "enc", [(i, i ^ 1) for i in range(16)])


def share_permute(v):
    pairs = []
    for y in range(SIDE):
        for x in range(SIDE):
            for e in range(16):
                to = (y + 2 * (e % 2) - 1) % SIDE
                pairs.append(((y * SIDE + x) * 16 + e, (to * SIDE + x) * 16 + e))
    return lax.ppermute(v, ("seq", "enc"), pairs)


def z_permute(v, shift):
    pairs = [(2 * z + c, 2 * ((z + shift) % 8) + c) for z in range(8) for c in range(2)]
    return lax.ppermute(v, "enc", pairs)


def z_partner(v):
    return lax.ppermute(v, "enc", [(2 * z + c, 2 * (z ^ 1) + c) for z in range(8) for c in range(2)])


def after_kernel(*refs):
    pass


def after(v, *others, flops=0):
    anywhere = pl.BlockSpec(memory_space=pl.ANY)
    return pl.pallas_call(
        after_kernel,
        in_specs=[anywhere] * (1 + len(others)),
        out_specs=anywhere,
        out_shape=jax.ShapeDtypeStruct(v.shape, v.dtype),
        input_output_aliases={0: 0},
        cost_estimate=pl.CostEstimate(flops=flops, bytes_accessed=0, transcendentals=0),
        name="after",
    )(v, *others)


def body(rows, wq, states, wk, wv, block_owner, block_index, out_grad):
    s = lax.axis_index("seq")
    e = lax.axis_index("enc")
    y = s // SIDE
    x = s % SIDE
    core = e % 2
    pos = jnp.stack([s, e, core, y, x, e // 2]).astype(jnp.int32)
    groups = 16
    refs = 64
    width = states.shape[-1]
    owner_all = block_owner.reshape(groups, refs)
    index_all = block_index.reshape(groups, refs)

    x1 = seq_permute(rows[0], x_perm(-1))
    x3 = seq_permute(rows[0], x_perm(1))
    xs = [rows[0], x1, seq_permute(x3[:64], x_perm(1)), seq_permute(x1[64:], x_perm(-1)), x3]
    near_w = share_permute(wq)
    half = wq.shape[0] // 2
    far_w = share_permute(lax.dynamic_slice(near_w, (core * half, 0), (half, HD)))
    ws = [wq, near_w, swap(near_w), far_w, swap(far_w)]
    send = pack(pos, owner_all, index_all, states)
    got = lax.all_to_all(send, "enc", 0, 0, tiled=True).reshape(groups * CAP, 8, width)
    og = out_grad[0]
    og = jnp.concatenate([og[SPAN - 1 :], jnp.zeros((SPAN - 1, HD), BF)], axis=0).reshape(SIDE, 512, HD)
    ogr = [lax.dynamic_index_in_dim(og, y, 0, keepdims=False)]
    for r in range(1, SIDE):
        piece = lax.dynamic_index_in_dim(og, (y + r) % SIDE, 0, keepdims=False)
        ogr.append(seq_permute(piece, y_perm(r)))
    qabs, qhead = vmem_call(
        query_kernel, [((SIDE, 512, HD), BF), ((SIDE, SPAN, HD), BF)], "queries", 14000000000, 9 << 20,
        pos, *xs, *ws, first=tuple(ogr[1:]),
    )

    w_kind = jnp.where(core == 0, wk, wv)
    w_all = lax.all_gather(w_kind, "seq", axis=0, tiled=False)

    owner_hot = (owner_all[:, :, None] == jnp.arange(groups, dtype=jnp.int32)).astype(jnp.int32)
    earlier = jnp.cumsum(owner_hot, axis=1) - owner_hot
    position = jnp.sum(earlier * owner_hot, axis=2)
    slot_ids = jnp.arange(CAP, dtype=jnp.int32)
    matched = (
        (owner_all == e)[:, :, None] & (position[:, :, None] == slot_ids[None, None, :])
    ).astype(jnp.int32)
    send_block = jnp.sum(matched * index_all[:, :, None], axis=1).reshape(-1)
    filled = jnp.sum(matched, axis=1).reshape(-1)
    my_owner = lax.dynamic_index_in_dim(owner_all, e, 0, keepdims=False)
    my_position = lax.dynamic_index_in_dim(position, e, 0, keepdims=False)
    recv_slot = my_owner * CAP + my_position
    slot_hot = (recv_slot[None, :] == jnp.arange(groups * CAP, dtype=jnp.int32)[:, None]).astype(jnp.int32)
    slot_ref = jnp.sum(slot_hot * jnp.arange(refs, dtype=jnp.int32)[None, :], axis=1)

    near = jnp.take(after(got, qabs), recv_slot, axis=0, mode="clip").reshape(groups, 32, width)
    near_all = lax.all_to_all(near, "seq", 0, 0, tiled=True).reshape(16, 2, 16, width)

    halo = seq_permute(qhead, y_perm(-1))
    sends = vmem_call(
        window_kernel, [((2, SIDE, 128, HD), BF)] * SIDE, "windows", 1 << 20, 3 << 20, pos, qabs, halo, *ogr
    )
    pieces = [sends[0]] + [seq_permute(sends[k], x_perm(-k)) for k in range(1, SIDE)]
    w_all = after(w_all, near_all, *pieces[1:])
    w_swap = swap(w_all)
    w_mine = [w_all.reshape(SIDE, SIDE, width, HD)]
    w_other = [w_swap.reshape(SIDE, SIDE, width, HD)]
    qo = jnp.stack(pieces)

    mine_a, other_a, mine_b, other_b, part = attention(pos, qo, w_mine, w_other, near_all)

    part = lax.all_to_all(part, "seq", 0, 0, tiled=True)

    def total(parts):
        return sum(p.astype(F32) for p in parts).astype(BF)

    other_a = swap(other_a)
    other_b = swap(other_b)
    ca = [total([mine_a[k], other_a[k]]) for k in range(SIDE)]
    cb = [total([mine_b[k], other_b[k]]) for k in range(SIDE)]
    ra = [ca[0]] + [seq_permute(ca[k], x_perm(k)) for k in (1, 3, 2)]
    rb = [cb[0]] + [seq_permute(cb[k], y_perm(k)) for k in (1, 3, 2)]

    part = after(part, ca[1], cb[1])
    att = part[:, 224:].reshape(2048, HD)
    attended = jnp.concatenate([jnp.zeros((SPAN - 1, HD), BF), att[: 2048 - SPAN + 1]], axis=0)
    part = part[:, :224].reshape(16, 2, 7, 2, 8, HD).transpose(0, 1, 3, 2, 4, 5).reshape(refs, 56, HD)
    back = jnp.take(part, slot_ref, axis=0, mode="clip").reshape(groups, CAP * 56, HD)
    back = lax.all_to_all(back, "enc", 0, 0, tiled=True).reshape(groups * CAP, 56, HD)
    block_hot = (
        (send_block[None, :] == jnp.arange(16, dtype=jnp.int32)[:, None]) & (filled[None, :] > 0)
    ).astype(BF)
    states_grad = lax.dot_general(block_hot, back, NN, preferred_element_type=F32).astype(BF)
    states_grad = states_grad.reshape(16, 7, 8, HD).transpose(0, 2, 1, 3).reshape(16, 8, width)

    ra, rb = total(ra), total(rb)
    parts = [ra[0]] + [seq_permute(ra[k], y_perm(k)) for k in range(1, SIDE)]
    parts += [rb[0]] + [seq_permute(rb[k], x_perm(k)) for k in range(1, SIDE)]
    slices = plane_sum(pos, parts)
    slices = [slices[0]] + [z_permute(slices[k], 2 * k) for k in range(1, 4)]
    keep, give = vmem_call(quarter_kernel, [((16, width), BF)] * 2, "quarter", 1 << 17, 1 << 18, pos, *slices, first=(back,))
    mine = vmem_call(eighth_kernel, [((16, width), BF)], "eighth", 1 << 17, 1 << 17, pos, keep, z_partner(give))[0]
    mine = vmem_call(pair_kernel, [((32, width), BF)], "pair", 1, 1 << 17, pos, mine, z_partner(mine))[0]
    spread = [mine] + [z_permute(mine, -2 * k) for k in range(1, 4)]
    mine = vmem_call(join_kernel, [((128, width), BF)], "join", 1, 1 << 19, pos, *spread)[0]
    key_grad, value_grad = vmem_call(
        final_kernel, [((width, HD), F32)] * 2, "final", 1, 3 << 19, pos, mine, swap(mine)
    )
    return attended[None], states_grad, key_grad, value_grad


def solution(mesh):
    placed = (
        P("enc", "seq", None),
        P(None, "seq"),
        P("enc", None, None),
        P(None, "seq"),
        P(None, "seq"),
        P(),
        P(),
        P("enc", None, "seq"),
    )
    return jax.shard_map(
        body,
        mesh=mesh,
        in_specs=placed,
        out_specs=(P("enc", None, "seq"), P("enc", "seq", None), P(None, "seq"), P(None, "seq")),
        check_vma=False,
    )
```

```python
import math

import jax
import jax.numpy as jnp
from jax import lax
from jax.experimental import pallas as pl
from jax.experimental.pallas import tpu as pltpu
from jax.sharding import PartitionSpec as P

HD = 128
SPAN = 64
NEIGH = 2
CAP = 5
SIDE = 4
BF = jnp.bfloat16
F32 = jnp.float32
NT = (((1,), (1,)), ((), ()))
TN = (((0,), (0,)), ((), ()))
NN = (((1,), (0,)), ((), ()))


def dot(a, b, dims):
    return lax.dot_general(a, b, dims, preferred_element_type=F32)


def x_perm(shift):
    return [(y * SIDE + x, y * SIDE + (x + shift) % SIDE) for y in range(SIDE) for x in range(SIDE)]


def y_perm(shift):
    return [(y * SIDE + x, ((y + shift) % SIDE) * SIDE + x) for y in range(SIDE) for x in range(SIDE)]


def pack_kernel(pos_ref, owner_ref, index_ref, tok_ref, out_ref):
    here = pos_ref[1]
    groups, refs = owner_ref.shape
    rows = groups * CAP * 8
    hot = owner_ref[...] == here
    before = lax.broadcasted_iota(jnp.int32, (refs, refs), 0) < lax.broadcasted_iota(jnp.int32, (refs, refs), 1)
    position = dot(hot.astype(BF), before.astype(BF), NN)
    position = jnp.where(hot, position, -1.0).astype(BF)
    row = lax.broadcasted_iota(jnp.int32, (rows, groups), 0)
    group_hot = (row // (CAP * 8) == lax.broadcasted_iota(jnp.int32, (rows, groups), 1)).astype(BF)
    position_row = dot(group_hot, position, NN)
    index_row = dot(group_hot, index_ref[...].astype(BF), NN)
    wide = lax.broadcasted_iota(jnp.int32, (rows, refs), 0)
    slot = ((wide // 8) % CAP).astype(F32)
    block = jnp.sum(jnp.where(position_row == slot, index_row + 1.0, 0.0), axis=1, keepdims=True) - 1.0
    pick_row = lax.broadcasted_iota(jnp.int32, (rows, 128), 0)
    pick_col = lax.broadcasted_iota(jnp.int32, (rows, 128), 1)
    pick = (block == (pick_col // 8).astype(F32)) & (pick_row % 8 == pick_col % 8)
    tok = tok_ref[...].reshape(128, tok_ref.shape[-1])
    out_ref[...] = dot(pick.astype(BF), tok, NN).astype(BF).reshape(out_ref.shape)


def pack(pos, owner, index, states):
    groups, refs = owner.shape
    width = states.shape[-1]
    return pl.pallas_call(
        pack_kernel,
        grid_spec=pltpu.PrefetchScalarGridSpec(
            num_scalar_prefetch=1,
            grid=(1,),
            in_specs=[
                pl.BlockSpec((groups, refs), lambda i, p: (0, 0)),
                pl.BlockSpec((groups, refs), lambda i, p: (0, 0)),
                pl.BlockSpec((16, 8, width), lambda i, p: (0, p[0], 0)),
            ],
            out_specs=pl.BlockSpec((groups, CAP * 8, width), lambda i, p: (0, 0, 0)),
        ),
        out_shape=jax.ShapeDtypeStruct((groups, CAP * 8, width), BF),
        cost_estimate=pl.CostEstimate(flops=150_000_000, bytes_accessed=2 << 20, transcendentals=0),
        name="pack_states",
    )(pos, owner, index, states)


def query_kernel(pos_ref, x0, x1, x2a, x2b, x3, own, near, near_other, far, far_other, out_ref, head_ref):
    core, y, x = pos_ref[2], pos_ref[3], pos_ref[4]
    first = core == 0
    low = jnp.where(first, far[...], far_other[...])
    high = jnp.where(first, far_other[...], far[...])
    across = jnp.concatenate([low, high], axis=0)
    weights = jnp.concatenate([own[...], near[...], across, near_other[...]], axis=1)
    rows = jnp.concatenate([r[...] for r in (x0, x1, x2a, x2b, x3)], axis=0)
    q = dot(rows, weights, NN).astype(BF)
    steps = (0, 1 + 2 * core, 2, 3 - 2 * core)
    for k in range(SIDE):
        tok = pl.multiple_of(lax.rem(x + k, SIDE) * 128, 128)
        for n in range(SIDE):
            head = lax.rem(y + steps[n], SIDE)
            out_ref[head, pl.ds(tok, 128), :] = q[128 * k : 128 * (k + 1), HD * n : HD * (n + 1)]
    head_ref[...] = out_ref[:, :SPAN, :]


def window_kernel(pos_ref, q_ref, halo_ref, o0, o1, o2, o3, p0, p1, p2, p3):
    y, x = pos_ref[3], pos_ref[4]
    halo = jnp.where(y == SIDE - 1, 0.0, halo_ref[...].astype(F32))
    for k, out_ref in enumerate((p0, p1, p2, p3)):
        to = lax.rem(x + SIDE - k, SIDE)
        start = pl.multiple_of(to * 128, 128)
        after_start = pl.multiple_of(lax.rem(to + 1, SIDE) * 128, 128)
        for j in range(SIDE):
            block = q_ref[j, pl.ds(start, 128), :].astype(F32)
            following = q_ref[j, pl.ds(after_start, SPAN), :].astype(F32)
            following = jnp.where(to == SIDE - 1, halo[j], following)
            rows = jnp.concatenate([block, following], axis=0)
            out_ref[0, j] = rows[SPAN - 1 : SPAN + 127].astype(BF)
        for r, o_ref in enumerate((o0, o1, o2, o3)):
            out_ref[1, lax.rem(y + SIDE - r, SIDE)] = o_ref[pl.ds(start, 128), :]


def vmem_call(kernel, outs, name, flops, nbytes, scalars, *arrays, first=()):
    whole = pl.BlockSpec(memory_space=pltpu.VMEM)
    count = 1 + len(arrays)

    def run(*refs):
        kernel(*refs[:count], *refs[count + len(first) :])

    return pl.pallas_call(
        run,
        in_specs=[pl.BlockSpec(memory_space=pltpu.SMEM)]
        + [whole] * len(arrays)
        + [pl.BlockSpec(memory_space=pl.ANY)] * len(first),
        out_specs=[whole] * len(outs),
        out_shape=[jax.ShapeDtypeStruct(shape, dtype) for shape, dtype in outs],
        compiler_params=pltpu.CompilerParams(vmem_limit_bytes=48 * 1024 * 1024),
        cost_estimate=pl.CostEstimate(flops=flops, bytes_accessed=nbytes, transcendentals=0),
        name=name,
    )(scalars, *arrays, *first)


def attend_kernel(pos_ref, qo_ref, *refs):
    mine_ref, other_ref, st_ref, ma_ref, oa_ref, mb_ref, ob_ref, part_ref, acc_ref, kt_ref = refs
    step = pl.program_id(0)
    factor = 1.0 / math.sqrt(HD)
    first = pos_ref[2] == 0
    y = pos_ref[3]
    qs, os, wvs, qp, op = [], [], [], [], []
    for n in range(SIDE):
        j = lax.rem(y + n, SIDE)
        m = mine_ref[j, 0]
        o = other_ref[j, 0]
        wk = jnp.where(first, m, o)
        wvs.append(jnp.where(first, o, m))
        qs.append(qo_ref[0, 0, j])
        os.append(qo_ref[0, 1, j])
        qp.append(dot(qs[n], wk, NT).astype(BF))
        op.append(dot(os[n], wvs[n], NT).astype(BF))

    @pl.when(step == 0)
    def _():
        acc_ref[...] = jnp.zeros_like(acc_ref)

    half = SIDE * SPAN
    @pl.when(step == 0)
    def _():
        for c in range(2):
            kt_ref[c] = st_ref[:, c].reshape(256, st_ref.shape[-1]).T

    ut = []
    for c in range(2):
        rows = slice(c * SPAN, (c + 1) * SPAN)
        lhs = jnp.concatenate([v[rows] for v in qp] + [v[rows] for v in op], axis=0)
        keys = st_ref[:, c].reshape(256, st_ref.shape[-1])
        both = dot(lhs, kt_ref[c], NN)
        pg = both[half:]
        raised = jnp.exp(both[:half] * factor)
        prob = raised / jnp.sum(raised, axis=1, keepdims=True)
        inner = jnp.sum(prob * pg, axis=1, keepdims=True)
        pb = prob.astype(BF)
        ds = (prob * (pg - inner) * factor).astype(BF)
        ut.append(dot(jnp.concatenate([pb, ds], axis=0), keys, NN).astype(BF))
        acc_ref[c] += dot(jnp.concatenate([ds, pb], axis=0), lhs, TN)

    for n in range(SIDE):
        rows = slice(n * SPAN, (n + 1) * SPAN)
        trows = slice(half + n * SPAN, half + (n + 1) * SPAN)
        u = jnp.concatenate([ut[0][rows], ut[1][rows]], axis=0)
        t = jnp.concatenate([ut[0][trows], ut[1][trows]], axis=0)
        head = lax.rem(y + n, SIDE) * SIDE + lax.rem(pos_ref[4] + step, SIDE)
        part_ref[head, 224:, :] = dot(u, wvs[n], NN).astype(BF)
        vg = dot(os[n], u, TN).astype(BF)
        kg = dot(qs[n], t, TN).astype(BF)
        mine = jnp.where(first, kg, vg)
        other = jnp.where(first, vg, kg)
        ma_ref[0, n] = mine[:SPAN]
        oa_ref[0, n] = other[:SPAN]
        mb_ref[n, 0] = mine[SPAN:]
        ob_ref[n, 0] = other[SPAN:]

    @pl.when(step == pl.num_programs(0) - 1)
    def _():
        for c in range(2):
            for f in range(7):
                rows = slice((c * 7 + f) * 16, (c * 7 + f) * 16 + 16)
                part_ref[:, rows, :] = acc_ref[c, :, f * 128 : (f + 1) * 128].astype(BF).reshape(16, 16, 128)


def attention(pos, qo, mine, other, states):
    width = states.shape[-1]
    w_spec = pl.BlockSpec((SIDE, 1, width, HD), lambda i, c: (0, lax.rem(c[4] + i, SIDE), 0, 0))
    st_spec = pl.BlockSpec((16, 2, 16, width), lambda i, c: (0, 0, 0, 0))
    a_spec = pl.BlockSpec((1, SIDE, SPAN, width), lambda i, c: (i, 0, 0, 0))
    b_spec = pl.BlockSpec((SIDE, 1, SPAN, width), lambda i, c: (0, i, 0, 0))
    grad = jax.ShapeDtypeStruct((SIDE, SIDE, SPAN, width), BF)
    return pl.pallas_call(
        attend_kernel,
        grid_spec=pltpu.PrefetchScalarGridSpec(
            num_scalar_prefetch=1,
            grid=(SIDE,),
            in_specs=[pl.BlockSpec((1, 2, SIDE, 128, HD), lambda i, c: (i, 0, 0, 0, 0))]
            + [w_spec] * 2
            + [st_spec],
            out_specs=[
                a_spec,
                a_spec,
                b_spec,
                b_spec,
                pl.BlockSpec((16, 352, HD), lambda i, c: (0, 0, 0)),
            ],
            scratch_shapes=[pltpu.VMEM((2, 256, width), F32), pltpu.VMEM((2, width, 256), BF)],
        ),
        out_shape=[
            grad,
            grad,
            grad,
            grad,
            jax.ShapeDtypeStruct((16, 352, HD), BF),
        ],
        compiler_params=pltpu.CompilerParams(vmem_limit_bytes=48 * 1024 * 1024),
        cost_estimate=pl.CostEstimate(flops=8_000_000_000, bytes_accessed=18 << 20, transcendentals=1 << 19),
        name="attend",
    )(pos, qo, *mine, *other, states)


def plane_kernel(pos_ref, *refs):
    outs, tmp = refs[8:12], refs[12]
    tmp[:SPAN] = sum(r[...].astype(F32) for r in refs[:4]).astype(BF)
    tmp[SPAN:] = sum(r[...].astype(F32) for r in refs[4:8]).astype(BF)
    pair = pos_ref[5] // 2
    for k in range(4):
        start = pl.multiple_of(lax.rem(pair + k, 4) * 32, 32)
        outs[k][...] = tmp[pl.ds(start, 32), :]


def plane_sum(pos, parts):
    width = parts[0].shape[-1]
    whole = pl.BlockSpec(memory_space=pltpu.VMEM)
    return pl.pallas_call(
        plane_kernel,
        in_specs=[pl.BlockSpec(memory_space=pltpu.SMEM)] + [whole] * 8,
        out_specs=[whole] * 4,
        out_shape=[jax.ShapeDtypeStruct((32, width), BF)] * 4,
        scratch_shapes=[pltpu.VMEM((128, width), BF)],
        cost_estimate=pl.CostEstimate(flops=10000000000, bytes_accessed=1 << 20, transcendentals=0),
        name="plane_sum",
    )(pos, *parts)


def quarter_kernel(pos_ref, r0, r1, r2, r3, out_ref):
    out_ref[...] = sum(r[...].astype(F32) for r in (r0, r1, r2, r3)).astype(BF)


def pair_kernel(pos_ref, mine_ref, got_ref, out_ref):
    out_ref[...] = (mine_ref[...].astype(F32) + got_ref[...].astype(F32)).astype(BF)


def join_kernel(pos_ref, r0, r1, r2, r3, out_ref):
    pair = pos_ref[5] // 2
    for k, r in enumerate((r0, r1, r2, r3)):
        start = pl.multiple_of(lax.rem(pair + k, 4) * 32, 32)
        out_ref[pl.ds(start, 32), :] = r[...]


def final_kernel(pos_ref, mine_ref, other_ref, key_ref, value_ref):
    first = pos_ref[2] == 0
    m = mine_ref[...]
    o = other_ref[...]
    key_ref[...] = jnp.where(first, m, o).astype(F32).T
    value_ref[...] = jnp.where(first, o, m).astype(F32).T


def seq_permute(v, perm):
    return lax.ppermute(v, "seq", perm)


def swap(v):
    return lax.ppermute(v, "enc", [(i, i ^ 1) for i in range(16)])


def share_permute(v):
    pairs = []
    for y in range(SIDE):
        for x in range(SIDE):
            for e in range(16):
                to = (y + 2 * (e % 2) - 1) % SIDE
                pairs.append(((y * SIDE + x) * 16 + e, (to * SIDE + x) * 16 + e))
    return lax.ppermute(v, ("seq", "enc"), pairs)


def z_permute(v, shift):
    pairs = [(2 * z + c, 2 * ((z + shift) % 8) + c) for z in range(8) for c in range(2)]
    return lax.ppermute(v, "enc", pairs)


def z_partner(v):
    return lax.ppermute(v, "enc", [(2 * z + c, 2 * (z ^ 1) + c) for z in range(8) for c in range(2)])


def after_kernel(*refs):
    pass


def after(v, *others, flops=0):
    anywhere = pl.BlockSpec(memory_space=pl.ANY)
    return pl.pallas_call(
        after_kernel,
        in_specs=[anywhere] * (1 + len(others)),
        out_specs=anywhere,
        out_shape=jax.ShapeDtypeStruct(v.shape, v.dtype),
        input_output_aliases={0: 0},
        cost_estimate=pl.CostEstimate(flops=flops, bytes_accessed=0, transcendentals=0),
        name="after",
    )(v, *others)


def body(rows, wq, states, wk, wv, block_owner, block_index, out_grad):
    s = lax.axis_index("seq")
    e = lax.axis_index("enc")
    y = s // SIDE
    x = s % SIDE
    core = e % 2
    pos = jnp.stack([s, e, core, y, x, e // 2]).astype(jnp.int32)
    groups = 16
    refs = 64
    width = states.shape[-1]
    owner_all = block_owner.reshape(groups, refs)
    index_all = block_index.reshape(groups, refs)

    x1 = seq_permute(rows[0], x_perm(-1))
    x3 = seq_permute(rows[0], x_perm(1))
    xs = [rows[0], x1, seq_permute(x3[:64], x_perm(1)), seq_permute(x1[64:], x_perm(-1)), x3]
    near_w = share_permute(wq)
    half = wq.shape[0] // 2
    far_w = share_permute(lax.dynamic_slice(near_w, (core * half, 0), (half, HD)))
    ws = [wq, near_w, swap(near_w), far_w, swap(far_w)]
    send = pack(pos, owner_all, index_all, states)
    got = lax.all_to_all(send, "enc", 0, 0, tiled=True).reshape(groups * CAP, 8, width)
    og = out_grad[0]
    og = jnp.concatenate([og[SPAN - 1 :], jnp.zeros((SPAN - 1, HD), BF)], axis=0).reshape(SIDE, 512, HD)
    ogr = [lax.dynamic_index_in_dim(og, y, 0, keepdims=False)]
    for r in range(1, SIDE):
        piece = lax.dynamic_index_in_dim(og, (y + r) % SIDE, 0, keepdims=False)
        ogr.append(seq_permute(piece, y_perm(r)))
    qabs, qhead = vmem_call(
        query_kernel, [((SIDE, 512, HD), BF), ((SIDE, SPAN, HD), BF)], "queries", 14000000000, 9 << 20,
        pos, *xs, *ws, first=tuple(ogr[1:]),
    )

    w_kind = jnp.where(core == 0, wk, wv)
    w_all = lax.all_gather(w_kind, "seq", axis=0, tiled=False)

    owner_hot = (owner_all[:, :, None] == jnp.arange(groups, dtype=jnp.int32)).astype(jnp.int32)
    earlier = jnp.cumsum(owner_hot, axis=1) - owner_hot
    position = jnp.sum(earlier * owner_hot, axis=2)
    slot_ids = jnp.arange(CAP, dtype=jnp.int32)
    matched = (
        (owner_all == e)[:, :, None] & (position[:, :, None] == slot_ids[None, None, :])
    ).astype(jnp.int32)
    send_block = jnp.sum(matched * index_all[:, :, None], axis=1).reshape(-1)
    filled = jnp.sum(matched, axis=1).reshape(-1)
    my_owner = lax.dynamic_index_in_dim(owner_all, e, 0, keepdims=False)
    my_position = lax.dynamic_index_in_dim(position, e, 0, keepdims=False)
    recv_slot = my_owner * CAP + my_position
    slot_hot = (recv_slot[None, :] == jnp.arange(groups * CAP, dtype=jnp.int32)[:, None]).astype(jnp.int32)
    slot_ref = jnp.sum(slot_hot * jnp.arange(refs, dtype=jnp.int32)[None, :], axis=1)

    near = jnp.take(after(got, qabs), recv_slot, axis=0, mode="clip").reshape(groups, 32, width)
    near_all = lax.all_to_all(near, "seq", 0, 0, tiled=True).reshape(16, 2, 16, width)

    halo = seq_permute(qhead, y_perm(-1))
    sends = vmem_call(
        window_kernel, [((2, SIDE, 128, HD), BF)] * SIDE, "windows", 1 << 20, 3 << 20, pos, qabs, halo, *ogr
    )
    pieces = [sends[0]] + [seq_permute(sends[k], x_perm(-k)) for k in range(1, SIDE)]
    w_all = after(w_all, near_all, *pieces[1:])
    w_swap = swap(w_all)
    w_mine = [w_all.reshape(SIDE, SIDE, width, HD)]
    w_other = [w_swap.reshape(SIDE, SIDE, width, HD)]
    qo = jnp.stack(pieces)

    mine_a, other_a, mine_b, other_b, part = attention(pos, qo, w_mine, w_other, near_all)

    part = lax.all_to_all(part, "seq", 0, 0, tiled=True)

    def total(parts):
        return sum(p.astype(F32) for p in parts).astype(BF)

    other_a = swap(other_a)
    other_b = swap(other_b)
    ca = [total([mine_a[k], other_a[k]]) for k in range(SIDE)]
    cb = [total([mine_b[k], other_b[k]]) for k in range(SIDE)]
    ra = [ca[0]] + [seq_permute(ca[k], x_perm(k)) for k in (1, 3, 2)]
    rb = [cb[0]] + [seq_permute(cb[k], y_perm(k)) for k in (1, 3, 2)]

    part = after(part, ca[1], cb[1])
    att = part[:, 224:].reshape(2048, HD)
    attended = jnp.concatenate([jnp.zeros((SPAN - 1, HD), BF), att[: 2048 - SPAN + 1]], axis=0)
    part = part[:, :224].reshape(16, 2, 7, 2, 8, HD).transpose(0, 1, 3, 2, 4, 5).reshape(refs, 56, HD)
    back = jnp.take(part, slot_ref, axis=0, mode="clip").reshape(groups, CAP * 56, HD)
    back = lax.all_to_all(back, "enc", 0, 0, tiled=True).reshape(groups * CAP, 56, HD)
    block_hot = (
        (send_block[None, :] == jnp.arange(16, dtype=jnp.int32)[:, None]) & (filled[None, :] > 0)
    ).astype(BF)
    states_grad = lax.dot_general(block_hot, back, NN, preferred_element_type=F32).astype(BF)
    states_grad = states_grad.reshape(16, 7, 8, HD).transpose(0, 2, 1, 3).reshape(16, 8, width)

    ra, rb = total(ra), total(rb)
    parts = [ra[0]] + [seq_permute(ra[k], y_perm(k)) for k in range(1, SIDE)]
    parts += [rb[0]] + [seq_permute(rb[k], x_perm(k)) for k in range(1, SIDE)]
    slices = plane_sum(pos, parts)
    slices = [slices[0]] + [z_permute(slices[k], 2 * k) for k in range(1, 4)]
    mine = vmem_call(
        quarter_kernel, [((32, width), BF)], "quarter", 1 << 17, 1 << 18, pos, *slices, first=(back,)
    )[0]
    mine = vmem_call(pair_kernel, [((32, width), BF)], "pair", 1 << 17, 1 << 18, pos, mine, z_partner(mine))[0]
    spread = [mine] + [z_permute(mine, -2 * k) for k in range(1, 4)]
    mine = vmem_call(join_kernel, [((128, width), BF)], "join", 1, 1 << 19, pos, *spread)[0]
    key_grad, value_grad = vmem_call(
        final_kernel, [((width, HD), F32)] * 2, "final", 1, 3 << 19, pos, mine, swap(mine)
    )
    return attended[None], states_grad, key_grad, value_grad


def solution(mesh):
    placed = (
        P("enc", "seq", None),
        P(None, "seq"),
        P("enc", None, None),
        P(None, "seq"),
        P(None, "seq"),
        P(),
        P(),
        P("enc", None, "seq"),
    )
    return jax.shard_map(
        body,
        mesh=mesh,
        in_specs=placed,
        out_specs=(P("enc", None, "seq"), P("enc", "seq", None), P(None, "seq"), P(None, "seq")),
        check_vma=False,
    )
```

```python
import math

import jax
import jax.numpy as jnp
from jax import lax
from jax.experimental import pallas as pl
from jax.experimental.pallas import tpu as pltpu
from jax.sharding import PartitionSpec as P

HD = 128
SPAN = 64
NEIGH = 2
CAP = 5
SIDE = 4
BF = jnp.bfloat16
F32 = jnp.float32
NT = (((1,), (1,)), ((), ()))
TN = (((0,), (0,)), ((), ()))
NN = (((1,), (0,)), ((), ()))


def dot(a, b, dims):
    return lax.dot_general(a, b, dims, preferred_element_type=F32)


def x_perm(shift):
    return [(y * SIDE + x, y * SIDE + (x + shift) % SIDE) for y in range(SIDE) for x in range(SIDE)]


def y_perm(shift):
    return [(y * SIDE + x, ((y + shift) % SIDE) * SIDE + x) for y in range(SIDE) for x in range(SIDE)]


def pack_kernel(pos_ref, owner_ref, index_ref, tok_ref, out_ref):
    here = pos_ref[1]
    groups, refs = owner_ref.shape
    rows = groups * CAP * 8
    hot = owner_ref[...] == here
    before = lax.broadcasted_iota(jnp.int32, (refs, refs), 0) < lax.broadcasted_iota(jnp.int32, (refs, refs), 1)
    position = dot(hot.astype(BF), before.astype(BF), NN)
    position = jnp.where(hot, position, -1.0).astype(BF)
    row = lax.broadcasted_iota(jnp.int32, (rows, groups), 0)
    group_hot = (row // (CAP * 8) == lax.broadcasted_iota(jnp.int32, (rows, groups), 1)).astype(BF)
    position_row = dot(group_hot, position, NN)
    index_row = dot(group_hot, index_ref[...].astype(BF), NN)
    wide = lax.broadcasted_iota(jnp.int32, (rows, refs), 0)
    slot = ((wide // 8) % CAP).astype(F32)
    block = jnp.sum(jnp.where(position_row == slot, index_row + 1.0, 0.0), axis=1, keepdims=True) - 1.0
    pick_row = lax.broadcasted_iota(jnp.int32, (rows, 128), 0)
    pick_col = lax.broadcasted_iota(jnp.int32, (rows, 128), 1)
    pick = (block == (pick_col // 8).astype(F32)) & (pick_row % 8 == pick_col % 8)
    tok = tok_ref[...].reshape(128, tok_ref.shape[-1])
    out_ref[...] = dot(pick.astype(BF), tok, NN).astype(BF).reshape(out_ref.shape)


def pack(pos, owner, index, states):
    groups, refs = owner.shape
    width = states.shape[-1]
    return pl.pallas_call(
        pack_kernel,
        grid_spec=pltpu.PrefetchScalarGridSpec(
            num_scalar_prefetch=1,
            grid=(1,),
            in_specs=[
                pl.BlockSpec((groups, refs), lambda i, p: (0, 0)),
                pl.BlockSpec((groups, refs), lambda i, p: (0, 0)),
                pl.BlockSpec((16, 8, width), lambda i, p: (0, p[0], 0)),
            ],
            out_specs=pl.BlockSpec((groups, CAP * 8, width), lambda i, p: (0, 0, 0)),
        ),
        out_shape=jax.ShapeDtypeStruct((groups, CAP * 8, width), BF),
        cost_estimate=pl.CostEstimate(flops=150_000_000, bytes_accessed=2 << 20, transcendentals=0),
        name="pack_states",
    )(pos, owner, index, states)


def query_kernel(pos_ref, x0, x1, x2a, x2b, x3, own, near, near_other, far, far_other, out_ref, head_ref):
    core, y, x = pos_ref[2], pos_ref[3], pos_ref[4]
    first = core == 0
    low = jnp.where(first, far[...], far_other[...])
    high = jnp.where(first, far_other[...], far[...])
    across = jnp.concatenate([low, high], axis=0)
    weights = jnp.concatenate([own[...], near[...], across, near_other[...]], axis=1)
    rows = jnp.concatenate([r[...] for r in (x0, x1, x2a, x2b, x3)], axis=0)
    q = dot(rows, weights, NN).astype(BF)
    steps = (0, 1 + 2 * core, 2, 3 - 2 * core)
    for k in range(SIDE):
        tok = pl.multiple_of(lax.rem(x + k, SIDE) * 128, 128)
        for n in range(SIDE):
            head = lax.rem(y + steps[n], SIDE)
            out_ref[head, pl.ds(tok, 128), :] = q[128 * k : 128 * (k + 1), HD * n : HD * (n + 1)]
    head_ref[...] = out_ref[:, :SPAN, :]


def window_kernel(pos_ref, q_ref, halo_ref, o0, o1, o2, o3, p0, p1, p2, p3):
    y, x = pos_ref[3], pos_ref[4]
    halo = jnp.where(y == SIDE - 1, 0.0, halo_ref[...].astype(F32))
    for k, out_ref in enumerate((p0, p1, p2, p3)):
        to = lax.rem(x + SIDE - k, SIDE)
        start = pl.multiple_of(to * 128, 128)
        after_start = pl.multiple_of(lax.rem(to + 1, SIDE) * 128, 128)
        for j in range(SIDE):
            block = q_ref[j, pl.ds(start, 128), :].astype(F32)
            following = q_ref[j, pl.ds(after_start, SPAN), :].astype(F32)
            following = jnp.where(to == SIDE - 1, halo[j], following)
            rows = jnp.concatenate([block, following], axis=0)
            out_ref[0, j] = rows[SPAN - 1 : SPAN + 127].astype(BF)
        for r, o_ref in enumerate((o0, o1, o2, o3)):
            out_ref[1, lax.rem(y + SIDE - r, SIDE)] = o_ref[pl.ds(start, 128), :]


def vmem_call(kernel, outs, name, flops, nbytes, scalars, *arrays, first=()):
    whole = pl.BlockSpec(memory_space=pltpu.VMEM)
    count = 1 + len(arrays)

    def run(*refs):
        kernel(*refs[:count], *refs[count + len(first) :])

    return pl.pallas_call(
        run,
        in_specs=[pl.BlockSpec(memory_space=pltpu.SMEM)]
        + [whole] * len(arrays)
        + [pl.BlockSpec(memory_space=pl.ANY)] * len(first),
        out_specs=[whole] * len(outs),
        out_shape=[jax.ShapeDtypeStruct(shape, dtype) for shape, dtype in outs],
        compiler_params=pltpu.CompilerParams(vmem_limit_bytes=48 * 1024 * 1024),
        cost_estimate=pl.CostEstimate(flops=flops, bytes_accessed=nbytes, transcendentals=0),
        name=name,
    )(scalars, *arrays, *first)


def attend_kernel(pos_ref, qo_ref, *refs):
    mine_ref, other_ref, st_ref, ma_ref, oa_ref, mb_ref, ob_ref, part_ref, acc_ref, kt_ref = refs
    step = pl.program_id(0)
    factor = 1.0 / math.sqrt(HD)
    first = pos_ref[2] == 0
    y = pos_ref[3]
    qs, os, wvs, qp, op = [], [], [], [], []
    for n in range(SIDE):
        j = lax.rem(y + n, SIDE)
        m = mine_ref[j, 0]
        o = other_ref[j, 0]
        wk = jnp.where(first, m, o)
        wvs.append(jnp.where(first, o, m))
        qs.append(qo_ref[0, 0, j])
        os.append(qo_ref[0, 1, j])
        qp.append(dot(qs[n], wk, NT).astype(BF))
        op.append(dot(os[n], wvs[n], NT).astype(BF))

    @pl.when(step == 0)
    def _():
        acc_ref[...] = jnp.zeros_like(acc_ref)

    half = SIDE * SPAN
    @pl.when(step == 0)
    def _():
        for c in range(2):
            kt_ref[c] = st_ref[:, c].reshape(256, st_ref.shape[-1]).T

    ut = []
    for c in range(2):
        rows = slice(c * SPAN, (c + 1) * SPAN)
        lhs = jnp.concatenate([v[rows] for v in qp] + [v[rows] for v in op], axis=0)
        keys = st_ref[:, c].reshape(256, st_ref.shape[-1])
        both = dot(lhs, kt_ref[c], NN)
        pg = both[half:]
        raised = jnp.exp(both[:half] * factor)
        prob = raised / jnp.sum(raised, axis=1, keepdims=True)
        inner = jnp.sum(prob * pg, axis=1, keepdims=True)
        pb = prob.astype(BF)
        ds = (prob * (pg - inner) * factor).astype(BF)
        ut.append(dot(jnp.concatenate([pb, ds], axis=0), keys, NN).astype(BF))
        acc_ref[c] += dot(jnp.concatenate([ds, pb], axis=0), lhs, TN)

    for n in range(SIDE):
        rows = slice(n * SPAN, (n + 1) * SPAN)
        trows = slice(half + n * SPAN, half + (n + 1) * SPAN)
        u = jnp.concatenate([ut[0][rows], ut[1][rows]], axis=0)
        t = jnp.concatenate([ut[0][trows], ut[1][trows]], axis=0)
        head = lax.rem(y + n, SIDE) * SIDE + lax.rem(pos_ref[4] + step, SIDE)
        part_ref[head, 224:, :] = dot(u, wvs[n], NN).astype(BF)
        vg = dot(os[n], u, TN).astype(BF)
        kg = dot(qs[n], t, TN).astype(BF)
        mine = jnp.where(first, kg, vg)
        other = jnp.where(first, vg, kg)
        ma_ref[0, n] = mine[:SPAN]
        oa_ref[0, n] = other[:SPAN]
        mb_ref[n, 0] = mine[SPAN:]
        ob_ref[n, 0] = other[SPAN:]

    @pl.when(step == pl.num_programs(0) - 1)
    def _():
        for c in range(2):
            for f in range(7):
                rows = slice((c * 7 + f) * 16, (c * 7 + f) * 16 + 16)
                part_ref[:, rows, :] = acc_ref[c, :, f * 128 : (f + 1) * 128].astype(BF).reshape(16, 16, 128)


def attention(pos, qo, mine, other, states):
    width = states.shape[-1]
    w_spec = pl.BlockSpec((SIDE, 1, width, HD), lambda i, c: (0, lax.rem(c[4] + i, SIDE), 0, 0))
    st_spec = pl.BlockSpec((16, 2, 16, width), lambda i, c: (0, 0, 0, 0))
    a_spec = pl.BlockSpec((1, SIDE, SPAN, width), lambda i, c: (i, 0, 0, 0))
    b_spec = pl.BlockSpec((SIDE, 1, SPAN, width), lambda i, c: (0, i, 0, 0))
    grad = jax.ShapeDtypeStruct((SIDE, SIDE, SPAN, width), BF)
    return pl.pallas_call(
        attend_kernel,
        grid_spec=pltpu.PrefetchScalarGridSpec(
            num_scalar_prefetch=1,
            grid=(SIDE,),
            in_specs=[pl.BlockSpec((1, 2, SIDE, 128, HD), lambda i, c: (i, 0, 0, 0, 0))]
            + [w_spec] * 2
            + [st_spec],
            out_specs=[
                a_spec,
                a_spec,
                b_spec,
                b_spec,
                pl.BlockSpec((16, 352, HD), lambda i, c: (0, 0, 0)),
            ],
            scratch_shapes=[pltpu.VMEM((2, 256, width), F32), pltpu.VMEM((2, width, 256), BF)],
        ),
        out_shape=[
            grad,
            grad,
            grad,
            grad,
            jax.ShapeDtypeStruct((16, 352, HD), BF),
        ],
        compiler_params=pltpu.CompilerParams(vmem_limit_bytes=48 * 1024 * 1024),
        cost_estimate=pl.CostEstimate(flops=8_000_000_000, bytes_accessed=18 << 20, transcendentals=1 << 19),
        name="attend",
    )(pos, qo, *mine, *other, states)


def plane_kernel(pos_ref, *refs):
    outs, tmp = refs[8:12], refs[12]
    tmp[:SPAN] = sum(r[...].astype(F32) for r in refs[:4]).astype(BF)
    tmp[SPAN:] = sum(r[...].astype(F32) for r in refs[4:8]).astype(BF)
    pair = pos_ref[5] // 2
    for k in range(4):
        start = pl.multiple_of(lax.rem(pair + k, 4) * 32, 32)
        outs[k][...] = tmp[pl.ds(start, 32), :]


def plane_sum(pos, parts):
    width = parts[0].shape[-1]
    whole = pl.BlockSpec(memory_space=pltpu.VMEM)
    return pl.pallas_call(
        plane_kernel,
        in_specs=[pl.BlockSpec(memory_space=pltpu.SMEM)] + [whole] * 8,
        out_specs=[whole] * 4,
        out_shape=[jax.ShapeDtypeStruct((32, width), BF)] * 4,
        scratch_shapes=[pltpu.VMEM((128, width), BF)],
        cost_estimate=pl.CostEstimate(flops=10000000000, bytes_accessed=1 << 20, transcendentals=0),
        name="plane_sum",
    )(pos, *parts)


def quarter_kernel(pos_ref, r0, r1, r2, r3, out_ref):
    out_ref[...] = sum(r[...].astype(F32) for r in (r0, r1, r2, r3)).astype(BF)


def pair_kernel(pos_ref, mine_ref, got_ref, out_ref):
    out_ref[...] = (mine_ref[...].astype(F32) + got_ref[...].astype(F32)).astype(BF)


def join_kernel(pos_ref, r0, r1, r2, r3, out_ref):
    pair = pos_ref[5] // 2
    for k, r in enumerate((r0, r1, r2, r3)):
        start = pl.multiple_of(lax.rem(pair + k, 4) * 32, 32)
        out_ref[pl.ds(start, 32), :] = r[...]


def final_kernel(pos_ref, mine_ref, other_ref, key_ref, value_ref):
    first = pos_ref[2] == 0
    m = mine_ref[...]
    o = other_ref[...]
    key_ref[...] = jnp.where(first, m, o).astype(F32).T
    value_ref[...] = jnp.where(first, o, m).astype(F32).T


def seq_permute(v, perm):
    return lax.ppermute(v, "seq", perm)


def swap(v):
    return lax.ppermute(v, "enc", [(i, i ^ 1) for i in range(16)])


def share_permute(v):
    pairs = []
    for y in range(SIDE):
        for x in range(SIDE):
            for e in range(16):
                to = (y + 2 * (e % 2) - 1) % SIDE
                pairs.append(((y * SIDE + x) * 16 + e, (to * SIDE + x) * 16 + e))
    return lax.ppermute(v, ("seq", "enc"), pairs)


def z_permute(v, shift):
    pairs = [(2 * z + c, 2 * ((z + shift) % 8) + c) for z in range(8) for c in range(2)]
    return lax.ppermute(v, "enc", pairs)


def z_partner(v):
    return lax.ppermute(v, "enc", [(2 * z + c, 2 * (z ^ 1) + c) for z in range(8) for c in range(2)])


def after_kernel(*refs):
    pass


def after(v, *others, flops=0):
    anywhere = pl.BlockSpec(memory_space=pl.ANY)
    return pl.pallas_call(
        after_kernel,
        in_specs=[anywhere] * (1 + len(others)),
        out_specs=anywhere,
        out_shape=jax.ShapeDtypeStruct(v.shape, v.dtype),
        input_output_aliases={0: 0},
        cost_estimate=pl.CostEstimate(flops=flops, bytes_accessed=0, transcendentals=0),
        name="after",
    )(v, *others)


def body(rows, wq, states, wk, wv, block_owner, block_index, out_grad):
    s = lax.axis_index("seq")
    e = lax.axis_index("enc")
    y = s // SIDE
    x = s % SIDE
    core = e % 2
    pos = jnp.stack([s, e, core, y, x, e // 2]).astype(jnp.int32)
    groups = 16
    refs = 64
    width = states.shape[-1]
    owner_all = block_owner.reshape(groups, refs)
    index_all = block_index.reshape(groups, refs)

    x1 = seq_permute(rows[0], x_perm(-1))
    x3 = seq_permute(rows[0], x_perm(1))
    xs = [rows[0], x1, seq_permute(x3[:64], x_perm(1)), seq_permute(x1[64:], x_perm(-1)), x3]
    near_w = share_permute(wq)
    half = wq.shape[0] // 2
    far_w = share_permute(lax.dynamic_slice(near_w, (core * half, 0), (half, HD)))
    ws = [wq, near_w, swap(near_w), far_w, swap(far_w)]
    send = pack(pos, owner_all, index_all, states)
    got = lax.all_to_all(send, "enc", 0, 0, tiled=True).reshape(groups * CAP, 8, width)
    og = out_grad[0]
    og = jnp.concatenate([og[SPAN - 1 :], jnp.zeros((SPAN - 1, HD), BF)], axis=0).reshape(SIDE, 512, HD)
    ogr = [lax.dynamic_index_in_dim(og, y, 0, keepdims=False)]
    for r in range(1, SIDE):
        piece = lax.dynamic_index_in_dim(og, (y + r) % SIDE, 0, keepdims=False)
        ogr.append(seq_permute(piece, y_perm(r)))
    qabs, qhead = vmem_call(
        query_kernel, [((SIDE, 512, HD), BF), ((SIDE, SPAN, HD), BF)], "queries", 14000000000, 9 << 20,
        pos, *xs, *ws, first=tuple(ogr[1:]),
    )

    w_kind = jnp.where(core == 0, wk, wv)
    w_all = lax.all_gather(w_kind, "seq", axis=0, tiled=False)

    owner_hot = (owner_all[:, :, None] == jnp.arange(groups, dtype=jnp.int32)).astype(jnp.int32)
    earlier = jnp.cumsum(owner_hot, axis=1) - owner_hot
    position = jnp.sum(earlier * owner_hot, axis=2)
    slot_ids = jnp.arange(CAP, dtype=jnp.int32)
    matched = (
        (owner_all == e)[:, :, None] & (position[:, :, None] == slot_ids[None, None, :])
    ).astype(jnp.int32)
    send_block = jnp.sum(matched * index_all[:, :, None], axis=1).reshape(-1)
    filled = jnp.sum(matched, axis=1).reshape(-1)
    my_owner = lax.dynamic_index_in_dim(owner_all, e, 0, keepdims=False)
    my_position = lax.dynamic_index_in_dim(position, e, 0, keepdims=False)
    recv_slot = my_owner * CAP + my_position
    slot_hot = (recv_slot[None, :] == jnp.arange(groups * CAP, dtype=jnp.int32)[:, None]).astype(jnp.int32)
    slot_ref = jnp.sum(slot_hot * jnp.arange(refs, dtype=jnp.int32)[None, :], axis=1)

    near = jnp.take(after(got, qabs), recv_slot, axis=0, mode="clip").reshape(groups, 32, width)
    near_all = lax.all_to_all(near, "seq", 0, 0, tiled=True).reshape(16, 2, 16, width)

    halo = seq_permute(qhead, y_perm(-1))
    sends = vmem_call(
        window_kernel, [((2, SIDE, 128, HD), BF)] * SIDE, "windows", 1 << 20, 3 << 20, pos, qabs, halo, *ogr
    )
    pieces = [sends[0]] + [seq_permute(sends[k], x_perm(-k)) for k in range(1, SIDE)]
    w_all = after(w_all, near_all, *pieces[1:])
    w_swap = swap(w_all)
    w_mine = [w_all.reshape(SIDE, SIDE, width, HD)]
    w_other = [w_swap.reshape(SIDE, SIDE, width, HD)]
    qo = jnp.stack(pieces)

    mine_a, other_a, mine_b, other_b, part = attention(pos, qo, w_mine, w_other, near_all)

    part = lax.all_to_all(part, "seq", 0, 0, tiled=True)

    def total(parts):
        return sum(p.astype(F32) for p in parts).astype(BF)

    other_a = swap(other_a)
    other_b = swap(other_b)
    ca = [None] + [total([mine_a[k], other_a[k]]) for k in range(1, SIDE)]
    cb = [None] + [total([mine_b[k], other_b[k]]) for k in range(1, SIDE)]
    ra = [mine_a[0], other_a[0]] + [seq_permute(ca[k], x_perm(k)) for k in (1, 3, 2)]
    rb = [mine_b[0], other_b[0]] + [seq_permute(cb[k], y_perm(k)) for k in (1, 3, 2)]

    part = after(part, ca[1], cb[1])
    att = part[:, 224:].reshape(2048, HD)
    attended = jnp.concatenate([jnp.zeros((SPAN - 1, HD), BF), att[: 2048 - SPAN + 1]], axis=0)
    part = part[:, :224].reshape(16, 2, 7, 2, 8, HD).transpose(0, 1, 3, 2, 4, 5).reshape(refs, 56, HD)
    back = jnp.take(part, slot_ref, axis=0, mode="clip").reshape(groups, CAP * 56, HD)
    back = lax.all_to_all(back, "enc", 0, 0, tiled=True).reshape(groups * CAP, 56, HD)
    block_hot = (
        (send_block[None, :] == jnp.arange(16, dtype=jnp.int32)[:, None]) & (filled[None, :] > 0)
    ).astype(BF)
    states_grad = lax.dot_general(block_hot, back, NN, preferred_element_type=F32).astype(BF)
    states_grad = states_grad.reshape(16, 7, 8, HD).transpose(0, 2, 1, 3).reshape(16, 8, width)

    ra, rb = total(ra), total(rb)
    parts = [ra[0]] + [seq_permute(ra[k], y_perm(k)) for k in range(1, SIDE)]
    parts += [rb[0]] + [seq_permute(rb[k], x_perm(k)) for k in range(1, SIDE)]
    slices = plane_sum(pos, parts)
    slices = [slices[0]] + [z_permute(slices[k], 2 * k) for k in range(1, 4)]
    mine = vmem_call(
        quarter_kernel, [((32, width), BF)], "quarter", 1 << 17, 1 << 18, pos, *slices, first=(back,)
    )[0]
    mine = vmem_call(pair_kernel, [((32, width), BF)], "pair", 1 << 17, 1 << 18, pos, mine, z_partner(mine))[0]
    spread = [mine] + [z_permute(mine, -2 * k) for k in range(1, 4)]
    mine = vmem_call(join_kernel, [((128, width), BF)], "join", 1, 1 << 19, pos, *spread)[0]
    key_grad, value_grad = vmem_call(
        final_kernel, [((width, HD), F32)] * 2, "final", 1, 3 << 19, pos, mine, swap(mine)
    )
    return attended[None], states_grad, key_grad, value_grad


def solution(mesh):
    placed = (
        P("enc", "seq", None),
        P(None, "seq"),
        P("enc", None, None),
        P(None, "seq"),
        P(None, "seq"),
        P(),
        P(),
        P("enc", None, "seq"),
    )
    return jax.shard_map(
        body,
        mesh=mesh,
        in_specs=placed,
        out_specs=(P("enc", None, "seq"), P("enc", "seq", None), P(None, "seq"), P(None, "seq")),
        check_vma=False,
    )
```
